32 devices in a mesh: sample: 16 (over z, x, core), space: 2 (over y).
Axes of the slice: x: 2, y: 2, z: 4, core: 2. Of those that a mesh axis runs over, the one named last changes fastest.
Arguments:
- volume: bfloat16 [16, 16, 16, 16, 128], P('sample', 'space'), may hold values from -6 to 6
- first_kernel: bfloat16 [3, 3, 3, 128, 128], replicated, may hold values from -0.109375 to 0.109375
- second_kernel: bfloat16 [3, 3, 3, 128, 128], replicated, may hold values from -0.109375 to 0.109375
- partner: int32 [16], replicated, may hold values from 0 to 15, as said below
- coefficient: float32 [16], replicated, may hold values from 0.25 to 0.75
- out_grad: bfloat16 [16, 16, 16, 16, 128], P('sample', 'space'), may hold values from -0.09375 to 0.09375
Outputs:
- result: bfloat16 [16, 16, 16, 16, 128], P('sample', 'space')
- first_kernel_grad: float32 [3, 3, 3, 128, 128], replicated
- second_kernel_grad: float32 [3, 3, 3, 128, 128], replicated
The draws below stay inside these ranges and needn't reach their ends.
Inputs may be any that keep to these rules, and one draw needn't show every extreme that they name: partner[partner[i]] == i and partner[i] != i for every sample i: the samples form pairs.
All inputs are finite; a program needn't handle non-finite values.
Results may differ from the reference program's by a relative error of at most 0.013.
Values may be sent and summed in bfloat16 or wider, within the bound.
A program may use at most 64 MiB of HBM per device.

```python
import jax
import jax.numpy as jnp
from jax import lax

C = 128
H = 16
W = 16
NB = 16
DEPTH = 16


def draw_partner(key, part):
    order = jax.random.permutation(jax.random.fold_in(key, 11), NB).astype(jnp.int32)
    leaders = order[0::2]
    followers = order[1::2]
    paired = jnp.zeros((NB,), jnp.int32)
    paired = paired.at[leaders].set(followers)
    paired = paired.at[followers].set(leaders)
    return paired


def block_levels(own_key, extent, pieces, smallest, largest):
    factor_of = 1.0
    for position, parts in pieces:
        heights = jax.random.uniform(jax.random.fold_in(jax.random.fold_in(own_key, 6), position), (parts,), jnp.float32, smallest / len(pieces), largest / len(pieces))
        factor_of = factor_of * jnp.repeat(jnp.exp(heights), extent[position] // parts).reshape((-1,) + (1,) * (len(extent) - 1 - position))
    return factor_of


def noise(rng, shape, deviation, bound, cuts=(), dtype=jnp.bfloat16):
    drawn = jax.random.normal(rng, shape, jnp.float32) * deviation
    if len(cuts) > 0:
        drawn = block_levels(rng, shape, cuts, -0.22, 0.18) * drawn
    return jnp.clip(drawn, min=-bound, max=bound).astype(dtype)


def setup_inputs(seed: int = 0) -> dict:
    key_list = jax.random.split(jax.random.key(seed), 7)
    return {
        "volume": noise(key_list[0], (NB, DEPTH, H, W, C), 1.0, 6.0, ((0, 16), (1, 2))),
        "first_kernel": noise(key_list[1], (3, 3, 3, C, C), (27 * C) ** -0.5, 0.109375),
        "second_kernel": noise(key_list[2], (3, 3, 3, C, C), (27 * C) ** -0.5, 0.109375),
        "partner": draw_partner(jax.random.fold_in(key_list[6], 71), 0),
        "coefficient": jnp.clip(jax.random.uniform(key_list[4], (NB,), jnp.float32, 0.25, 0.75), 0.25, 0.75),
        "out_grad": noise(key_list[5], (NB, DEPTH, H, W, C), (4.0 / (NB * DEPTH * H * W) ** 0.5), 0.09375, ((0, 16), (1, 2))),
    }


def convolve(volume_in, kernel, spread):
    return lax.conv_general_dilated(volume_in, kernel, (1, 1, 1), ((spread, spread), (spread, spread), (spread, spread)), rhs_dilation=(spread, spread, spread), dimension_numbers=("NDHWC", "DHWIO", "NDHWC"), precision=lax.Precision.HIGHEST)


def slope(value):
    squash = jax.nn.sigmoid(value)
    return squash * (1.0 + value * (1.0 - squash))


def tap_grads(source, cotangent, spread):
    sample_count, depth_size, row_size, col_size, chan_size = cotangent.shape
    framed = jnp.pad(source, ((0, 0), (spread, spread), (spread, spread), (spread, spread), (0, 0)))
    flat_cotangent = cotangent.reshape(-1, chan_size)
    plane_list = []
    for depth_tap in range(3):
        line_list = []
        for row_tap in range(3):
            tap_list = []
            for col_tap in range(3):
                window = lax.slice(framed, (0, depth_tap * spread, row_tap * spread, col_tap * spread, 0), (sample_count, depth_tap * spread + depth_size, row_tap * spread + row_size, col_tap * spread + col_size, framed.shape[4]))
                tap_list.append(jnp.dot(window.reshape(-1, framed.shape[4]).T, flat_cotangent, precision=lax.Precision.HIGHEST))
            line_list.append(jnp.stack(tap_list))
        plane_list.append(jnp.stack(line_list))
    return jnp.stack(plane_list)


def reference(volume, first_kernel, second_kernel, partner, coefficient, out_grad):
    inputs = volume.astype(jnp.float32)
    kernel_one = first_kernel.astype(jnp.float32)
    kernel_two = second_kernel.astype(jnp.float32)
    pre_one = convolve(inputs, kernel_one, 1)
    hidden = jax.nn.silu(pre_one).astype(jnp.bfloat16)
    hidden_wide = hidden.astype(jnp.float32)
    weight_self = coefficient[:, None, None, None, None]
    mixed = (weight_self * hidden_wide + (1.0 - weight_self) * hidden_wide[partner]).astype(jnp.bfloat16)
    mixed_wide = mixed.astype(jnp.float32)
    pre_two = convolve(mixed_wide, kernel_two, 2)
    result = jax.nn.silu(pre_two).astype(jnp.bfloat16)
    grad_two = (out_grad.astype(jnp.float32) * slope(pre_two)).astype(jnp.bfloat16)
    grad_two_wide = grad_two.astype(jnp.float32)
    second_kernel_grad = tap_grads(mixed_wide, grad_two_wide, 2)
    flipped = jnp.transpose(jnp.flip(kernel_two, (0, 1, 2)), (0, 1, 2, 4, 3))
    grad_mixed = convolve(grad_two_wide, flipped, 2)
    grad_mixed = lax.optimization_barrier(grad_mixed.astype(jnp.bfloat16)).astype(jnp.float32)
    weight_other = (1.0 - coefficient[partner])[:, None, None, None, None]
    grad_hidden = weight_self * grad_mixed + weight_other * grad_mixed[partner]
    grad_hidden = lax.optimization_barrier(grad_hidden.astype(jnp.bfloat16)).astype(jnp.float32)
    grad_one = (grad_hidden * slope(pre_one)).astype(jnp.bfloat16)
    first_kernel_grad = tap_grads(inputs, grad_one.astype(jnp.float32), 1)
    return result, first_kernel_grad, second_kernel_grad
```

```python
import functools

import jax
import jax.numpy as jnp
from jax import lax
from jax.experimental import pallas as pl
from jax.experimental.pallas import tpu as pltpu
from jax.sharding import PartitionSpec as P

F32 = jnp.float32
BF16 = jnp.bfloat16
VMEM_LIMIT = 56 * 1024 * 1024


def slope(value):
    squash = jax.nn.sigmoid(value)
    return squash * (1.0 + value * (1.0 - squash))


def groups(depth, spread):
    first = [p for p in range(depth) if (p // spread) % 2 == 0]
    return first, [p + spread for p in first]


def frame(store, layer, plane, spread, width):
    cells, chans = plane.shape
    edge = spread * width
    wide = plane.astype(F32)
    column = lax.broadcasted_iota(jnp.int32, plane.shape, 0) % width
    left = jnp.where(column >= spread, pltpu.roll(wide, spread, 0), 0.0).astype(BF16)
    right = jnp.where(column < width - spread, pltpu.roll(wide, cells - spread, 0), 0.0).astype(BF16)
    store[layer, pl.ds(0, edge), :] = jnp.zeros((edge, 3 * chans), BF16)
    store[layer, pl.ds(edge + cells, edge), :] = jnp.zeros((edge, 3 * chans), BF16)
    for place, value in enumerate((left, plane, right)):
        store[layer, pl.ds(edge, cells), pl.ds(place * chans, chans)] = value


def taps(store, layer, spread, width, cells):
    return jnp.concatenate(
        [store[layer, pl.ds(row * spread * width, cells), :] for row in range(3)], axis=1
    )


def fill_pairs(kernel_ref, wide_ref):
    chans = kernel_ref.shape[2]
    for step in range(4):
        for out in range(2):
            depth_tap = step - out
            block = (
                kernel_ref[depth_tap]
                if 0 <= depth_tap < 3
                else jnp.zeros(kernel_ref.shape[1:], BF16)
            )
            wide_ref[step, :, pl.ds(out * chans, chans)] = block


def conv_pairs(store, wide_ref, depth, spread, width, cells):
    chans = wide_ref.shape[2] // 2
    first, _ = groups(depth, spread)
    total = None
    for half in range(2):
        rows = []
        for p in first:
            rows.append(
                jnp.concatenate(
                    [
                        taps(store, p + spread * (2 * half + k), spread, width, cells)
                        for k in range(2)
                    ],
                    axis=1,
                )
            )
        lhs = jnp.concatenate(rows, axis=0)
        rhs = jnp.concatenate([wide_ref[2 * half], wide_ref[2 * half + 1]], axis=0)
        part = jnp.dot(lhs, rhs, preferred_element_type=F32)
        total = part if total is None else total + part
    for place, p in enumerate(first):
        for out in range(2):
            yield p + out * spread, total[
                place * cells : (place + 1) * cells, out * chans : (out + 1) * chans
            ]


def grad_blocks(store, grad_at, depth, spread, width, cells):
    ranges = ((0, 2 * spread, (0, 1)), (2 * spread, depth, (0, 1, 2)), (depth, depth + 2 * spread, (1, 2)))
    for low, high, depth_taps in ranges:
        lhs = jnp.concatenate(
            [taps(store, e, spread, width, cells) for e in range(low, high)], axis=0
        )
        columns = []
        for tap in depth_taps:
            layers = []
            for e in range(low, high):
                p = e - spread * tap
                layers.append(grad_at(p if 0 <= p < depth else None))
            columns.append(jnp.concatenate(layers, axis=0))
        rhs = jnp.concatenate(columns, axis=1)
        part = lax.dot_general(lhs, rhs, (((0,), (0,)), ((), ())), preferred_element_type=F32)
        chans = columns[0].shape[1]
        for place, tap in enumerate(depth_taps):
            yield tap, part[:, place * chans : (place + 1) * chans]


def first_kernel_body(width, share_ref, x_ref, kernel_ref, hidden_ref, slope_ref, store, wide_ref):
    depth, cells, _ = hidden_ref.shape
    for layer in range(depth + 2):
        frame(store, layer, x_ref[layer], 1, width)
    fill_pairs(kernel_ref, wide_ref)
    for p, value in conv_pairs(store, wide_ref, depth, 1, width, cells):
        squash = jax.nn.sigmoid(value)
        hidden_ref[p] = (value * squash).astype(BF16)
        slope_ref[p] = share_ref[0] * (squash * (1.0 + value * (1.0 - squash)))


def mix_body(width, share_ref, x_ref, kernel_ref, own_ref, mixed_ref, slope_ref, store, wide_ref):
    depth, cells, _ = mixed_ref.shape
    for layer in range(depth + 2):
        frame(store, layer, x_ref[layer], 1, width)
    fill_pairs(kernel_ref, wide_ref)
    for p, value in conv_pairs(store, wide_ref, depth, 1, width, cells):
        squash = jax.nn.sigmoid(value)
        hidden = (value * squash).astype(BF16).astype(F32)
        mixed_ref[p] = (share_ref[0] * own_ref[p].astype(F32) + share_ref[1] * hidden).astype(BF16)
        slope_ref[p] = share_ref[1] * (squash * (1.0 + value * (1.0 - squash)))


def second_body(width, low_ref, mixed_ref, high_ref, kernel_ref, cot_ref, result_ref, grad_ref, store, wide_ref):
    depth, cells, _ = result_ref.shape
    for layer in range(depth + 4):
        plane = (
            low_ref[layer]
            if layer < 2
            else (mixed_ref[layer - 2] if layer < depth + 2 else high_ref[layer - depth - 2])
        )
        frame(store, layer, plane, 2, width)
    fill_pairs(kernel_ref, wide_ref)
    for p, value in conv_pairs(store, wide_ref, depth, 2, width, cells):
        squash = jax.nn.sigmoid(value)
        result_ref[p] = (value * squash).astype(BF16)
        grad_ref[p] = (
            cot_ref[p].astype(F32) * (squash * (1.0 + value * (1.0 - squash)))
        ).astype(BF16)


def second_grad_body(width, low_ref, mixed_ref, high_ref, grad_ref, out_ref, store, total):
    depth, cells, chans = grad_ref.shape
    for layer in range(depth + 4):
        plane = (
            low_ref[layer]
            if layer < 2
            else (mixed_ref[layer - 2] if layer < depth + 2 else high_ref[layer - depth - 2])
        )
        frame(store, layer, plane, 2, width)

    def grad_at(p):
        return jnp.zeros((cells, chans), BF16) if p is None else grad_ref[p]

    total[...] = jnp.zeros_like(total)
    for tap, part in grad_blocks(store, grad_at, depth, 2, width, cells):
        total[tap] += part
    out_ref[...] = total[...].astype(BF16)


def back_body(
    width, low_ref, grad_ref, high_ref, kernel_ref, slope_own_ref, slope_mate_ref, own_ref, mate_ref,
    out_ref, store, wide_ref, term_own, term_mate, store_one, total,
):
    depth, cells, chans = grad_ref.shape
    for layer in range(depth + 4):
        plane = (
            low_ref[layer]
            if layer < 2
            else (grad_ref[layer - 2] if layer < depth + 2 else high_ref[layer - depth - 2])
        )
        frame(store, layer, plane, 2, width)
    fill_pairs(kernel_ref, wide_ref)
    for p, value in conv_pairs(store, wide_ref, depth, 2, width, cells):
        value = value.astype(BF16).astype(F32)
        term_own[p] = (value * slope_own_ref[p]).astype(BF16)
        term_mate[p] = (value * slope_mate_ref[p]).astype(BF16)
    total[...] = jnp.zeros_like(total)
    for x_ref, term in ((own_ref, term_own), (mate_ref, term_mate)):
        for layer in range(depth + 2):
            frame(store_one, layer, x_ref[layer], 1, width)

        def grad_at(p, term=term):
            return jnp.zeros((cells, chans), BF16) if p is None else term[p]

        for tap, part in grad_blocks(store_one, grad_at, depth, 1, width, cells):
            total[tap] += part
    out_ref[...] = total[...].astype(BF16)


def call(body, width, args, outs, scratch, flops, smem=0):
    vmem = pl.BlockSpec(memory_space=pltpu.VMEM)
    scalar = pl.BlockSpec(memory_space=pltpu.SMEM)
    size = sum(a.size * a.dtype.itemsize for a in args)
    return pl.pallas_call(
        functools.partial(body, width),
        out_shape=outs,
        in_specs=[scalar] * smem + [vmem] * (len(args) - smem),
        out_specs=jax.tree.map(lambda _: vmem, outs),
        scratch_shapes=scratch,
        compiler_params=pltpu.CompilerParams(vmem_limit_bytes=VMEM_LIMIT),
        cost_estimate=pl.CostEstimate(flops=flops, bytes_accessed=size, transcendentals=0),
    )(*args)


def edges(block, width):
    count = lax.axis_size("space")
    low = lax.ppermute(block[-width:], "space", [(i, i + 1) for i in range(count - 1)])
    high = lax.ppermute(block[:width], "space", [(i + 1, i) for i in range(count - 1)])
    return low, high


def shards(volume, first_kernel, second_kernel, partner, coefficient, out_grad):
    _, depth, height, width, chans = volume.shape
    cells = height * width
    me = lax.axis_index("sample")
    own_share = coefficient[me]
    shares = jnp.stack([own_share, 1.0 - own_share])
    x = volume.reshape(depth, cells, chans)
    cot = out_grad.reshape(depth, cells, chans)
    flat_one = first_kernel.reshape(3, 9 * chans, chans)
    flat_two = second_kernel.reshape(3, 9 * chans, chans)
    flipped = jnp.transpose(jnp.flip(second_kernel, (0, 1, 2)), (0, 1, 2, 4, 3)).reshape(
        3, 9 * chans, chans
    )
    count = lax.axis_size("sample")
    pieces = lax.all_to_all(
        x.reshape(count, depth * cells // count, chans), "sample", split_axis=0, concat_axis=0, tiled=True
    )
    mate = lax.all_to_all(
        jnp.take(pieces, partner, axis=0), "sample", split_axis=0, concat_axis=0, tiled=True
    ).reshape(depth, cells, chans)
    low, high = edges(x, 1)
    own_pad = jnp.concatenate([low, x, high], axis=0)
    low, high = edges(mate, 1)
    mate_pad = jnp.concatenate([low, mate, high], axis=0)
    layer = (depth, cells, chans)
    half = jax.ShapeDtypeStruct(layer, BF16)
    full = jax.ShapeDtypeStruct(layer, F32)
    unit = 2 * depth * cells * 27 * chans * chans
    store_one = pltpu.VMEM((depth + 2, cells + 2 * width, 3 * chans), BF16)
    store_two = pltpu.VMEM((depth + 4, cells + 4 * width, 3 * chans), BF16)
    wide = pltpu.VMEM((4, 9 * chans, 2 * chans), BF16)
    total = pltpu.VMEM((3, 9 * chans, chans), F32)
    hidden, slope_own = call(
        first_kernel_body, width, (shares, own_pad, flat_one), (half, full), [store_one, wide], unit, 1
    )
    mixed, slope_mate = call(
        mix_body, width, (shares, mate_pad, flat_one, hidden), (half, full), [store_one, wide], unit, 1
    )
    low, high = edges(mixed, 2)
    result, grad_two = call(
        second_body, width, (low, mixed, high, flat_two, cot), (half, half), [store_two, wide], unit
    )
    terms = jax.ShapeDtypeStruct((3, 9 * chans, chans), BF16)
    second_local = call(
        second_grad_body, width, (low, mixed, high, grad_two), terms, [store_two, total], unit
    )
    low, high = edges(grad_two, 2)
    first_local = call(
        back_body,
        width,
        (low, grad_two, high, flipped, slope_own, slope_mate, own_pad, mate_pad),
        terms,
        [store_two, wide, pltpu.VMEM(layer, BF16), pltpu.VMEM(layer, BF16), store_one, total],
        3 * unit,
    )
    shape = first_kernel.shape
    second_sum = lax.psum(second_local, ("sample", "space")).astype(F32).reshape(shape)
    first_sum = lax.psum(first_local, ("sample", "space")).astype(F32).reshape(shape)
    return result.reshape(volume.shape), first_sum, second_sum


def solution(mesh):
    in_specs = (
        P("sample", "space", None, None, None),
        P(),
        P(),
        P(),
        P(),
        P("sample", "space", None, None, None),
    )
    out_specs = (P("sample", "space", None, None, None), P(), P())
    return jax.shard_map(shards, mesh=mesh, in_specs=in_specs, out_specs=out_specs, check_vma=False)
```

```python
import functools

import jax
import jax.numpy as jnp
from jax import lax
from jax.experimental import pallas as pl
from jax.experimental.pallas import tpu as pltpu
from jax.sharding import PartitionSpec as P

F32 = jnp.float32
BF16 = jnp.bfloat16
VMEM_LIMIT = 56 * 1024 * 1024


def slope(value):
    squash = jax.nn.sigmoid(value)
    return squash * (1.0 + value * (1.0 - squash))


def groups(depth, spread):
    first = [p for p in range(depth) if (p // spread) % 2 == 0]
    return first, [p + spread for p in first]


def frame(store, layer, plane, spread, width):
    cells, chans = plane.shape
    edge = spread * width
    wide = plane.astype(F32)
    column = lax.broadcasted_iota(jnp.int32, plane.shape, 0) % width
    left = jnp.where(column >= spread, pltpu.roll(wide, spread, 0), 0.0).astype(BF16)
    right = jnp.where(column < width - spread, pltpu.roll(wide, cells - spread, 0), 0.0).astype(BF16)
    store[layer, pl.ds(0, edge), :] = jnp.zeros((edge, 3 * chans), BF16)
    store[layer, pl.ds(edge + cells, edge), :] = jnp.zeros((edge, 3 * chans), BF16)
    for place, value in enumerate((left, plane, right)):
        store[layer, pl.ds(edge, cells), pl.ds(place * chans, chans)] = value


def taps(store, layer, spread, width, cells):
    return jnp.concatenate(
        [store[layer, pl.ds(row * spread * width, cells), :] for row in range(3)], axis=1
    )


def fill_pairs(kernel_ref, wide_ref):
    chans = kernel_ref.shape[2]
    for step in range(4):
        for out in range(2):
            depth_tap = step - out
            block = (
                kernel_ref[depth_tap]
                if 0 <= depth_tap < 3
                else jnp.zeros(kernel_ref.shape[1:], BF16)
            )
            wide_ref[step, :, pl.ds(out * chans, chans)] = block


def conv_pairs(store, wide_ref, depth, spread, width, cells):
    chans = wide_ref.shape[2] // 2
    first, _ = groups(depth, spread)
    total = None
    for half in range(2):
        rows = []
        for p in first:
            rows.append(
                jnp.concatenate(
                    [
                        taps(store, p + spread * (2 * half + k), spread, width, cells)
                        for k in range(2)
                    ],
                    axis=1,
                )
            )
        lhs = jnp.concatenate(rows, axis=0)
        rhs = jnp.concatenate([wide_ref[2 * half], wide_ref[2 * half + 1]], axis=0)
        part = jnp.dot(lhs, rhs, preferred_element_type=F32)
        total = part if total is None else total + part
    for place, p in enumerate(first):
        for out in range(2):
            yield p + out * spread, total[
                place * cells : (place + 1) * cells, out * chans : (out + 1) * chans
            ]


def grad_blocks(store, grad_at, depth, spread, width, cells):
    ranges = ((0, 2 * spread, (0, 1)), (2 * spread, depth, (0, 1, 2)), (depth, depth + 2 * spread, (1, 2)))
    for low, high, depth_taps in ranges:
        lhs = jnp.concatenate(
            [taps(store, e, spread, width, cells) for e in range(low, high)], axis=0
        )
        columns = []
        for tap in depth_taps:
            layers = []
            for e in range(low, high):
                p = e - spread * tap
                layers.append(grad_at(p if 0 <= p < depth else None))
            columns.append(jnp.concatenate(layers, axis=0))
        rhs = jnp.concatenate(columns, axis=1)
        part = lax.dot_general(lhs, rhs, (((0,), (0,)), ((), ())), preferred_element_type=F32)
        chans = columns[0].shape[1]
        for place, tap in enumerate(depth_taps):
            yield tap, part[:, place * chans : (place + 1) * chans]


def frame_all(store, low_ref, x_ref, high_ref, spread, width):
    depth = x_ref.shape[0]
    for layer in range(depth + 2 * spread):
        if layer < spread:
            plane = low_ref[layer]
        elif layer < depth + spread:
            plane = x_ref[layer - spread]
        else:
            plane = high_ref[layer - depth - spread]
        frame(store, layer, plane, spread, width)


def first_kernel_body(width, share_ref, low_ref, x_ref, high_ref, kernel_ref, hidden_ref, slope_ref, store, wide_ref):
    depth, cells, _ = hidden_ref.shape
    frame_all(store, low_ref, x_ref, high_ref, 1, width)
    fill_pairs(kernel_ref, wide_ref)
    for p, value in conv_pairs(store, wide_ref, depth, 1, width, cells):
        squash = jax.nn.sigmoid(value)
        hidden_ref[p] = (value * squash).astype(BF16)
        slope_ref[p] = share_ref[0] * (squash * (1.0 + value * (1.0 - squash)))


def mix_body(width, share_ref, low_ref, x_ref, high_ref, kernel_ref, own_ref, mixed_ref, slope_ref, store, wide_ref):
    depth, cells, _ = mixed_ref.shape
    frame_all(store, low_ref, x_ref, high_ref, 1, width)
    fill_pairs(kernel_ref, wide_ref)
    for p, value in conv_pairs(store, wide_ref, depth, 1, width, cells):
        squash = jax.nn.sigmoid(value)
        hidden = (value * squash).astype(BF16).astype(F32)
        mixed_ref[p] = (share_ref[0] * own_ref[p].astype(F32) + share_ref[1] * hidden).astype(BF16)
        slope_ref[p] = share_ref[1] * (squash * (1.0 + value * (1.0 - squash)))


def second_body(width, low_ref, mixed_ref, high_ref, kernel_ref, cot_ref, result_ref, grad_ref, store, wide_ref):
    depth, cells, _ = result_ref.shape
    frame_all(store, low_ref, mixed_ref, high_ref, 2, width)
    fill_pairs(kernel_ref, wide_ref)
    for p, value in conv_pairs(store, wide_ref, depth, 2, width, cells):
        squash = jax.nn.sigmoid(value)
        result_ref[p] = (value * squash).astype(BF16)
        grad_ref[p] = (
            cot_ref[p].astype(F32) * (squash * (1.0 + value * (1.0 - squash)))
        ).astype(BF16)


def second_grad_body(width, low_ref, mixed_ref, high_ref, grad_ref, out_ref, store, total):
    depth, cells, chans = grad_ref.shape
    frame_all(store, low_ref, mixed_ref, high_ref, 2, width)

    def grad_at(p):
        return jnp.zeros((cells, chans), BF16) if p is None else grad_ref[p]

    total[...] = jnp.zeros_like(total)
    for tap, part in grad_blocks(store, grad_at, depth, 2, width, cells):
        total[tap] += part
    out_ref[...] = total[...].astype(BF16)


def back_body(
    width, low_ref, grad_ref, high_ref, kernel_ref, slope_own_ref, slope_mate_ref,
    own_low, own_ref, own_high, mate_low, mate_ref, mate_high, out_ref, store, wide_ref, term_own, term_mate, store_one, total,
):
    depth, cells, chans = grad_ref.shape
    frame_all(store, low_ref, grad_ref, high_ref, 2, width)
    fill_pairs(kernel_ref, wide_ref)
    for p, value in conv_pairs(store, wide_ref, depth, 2, width, cells):
        value = value.astype(BF16).astype(F32)
        term_own[p] = (value * slope_own_ref[p]).astype(BF16)
        term_mate[p] = (value * slope_mate_ref[p]).astype(BF16)
    total[...] = jnp.zeros_like(total)
    for faces, term in (((own_low, own_ref, own_high), term_own), ((mate_low, mate_ref, mate_high), term_mate)):
        frame_all(store_one, *faces, 1, width)

        def grad_at(p, term=term):
            return jnp.zeros((cells, chans), BF16) if p is None else term[p]

        for tap, part in grad_blocks(store_one, grad_at, depth, 1, width, cells):
            total[tap] += part
    out_ref[...] = total[...].astype(BF16)


def call(body, width, args, outs, scratch, flops, smem=0):
    vmem = pl.BlockSpec(memory_space=pltpu.VMEM)
    scalar = pl.BlockSpec(memory_space=pltpu.SMEM)
    size = sum(a.size * a.dtype.itemsize for a in args)
    return pl.pallas_call(
        functools.partial(body, width),
        out_shape=outs,
        in_specs=[scalar] * smem + [vmem] * (len(args) - smem),
        out_specs=jax.tree.map(lambda _: vmem, outs),
        scratch_shapes=scratch,
        compiler_params=pltpu.CompilerParams(vmem_limit_bytes=VMEM_LIMIT),
        cost_estimate=pl.CostEstimate(flops=flops, bytes_accessed=size, transcendentals=0),
    )(*args)


def neighbours(count):
    me = lax.axis_index("space")
    return (me > 0, {"space": me - 1}), (me < count - 1, {"space": me + 1})


def greet(peers, ends):
    barrier = pltpu.get_barrier_semaphore()
    for peer in peers:
        pl.semaphore_signal(barrier, inc=1, device_id=peer, device_id_type=pl.DeviceIdType.MESH)
    for exists, peer in ends:

        @pl.when(exists)
        def _(peer=peer):
            pl.semaphore_signal(barrier, inc=1, device_id=peer, device_id_type=pl.DeviceIdType.MESH)

    waits = len(peers)
    if ends:
        me = lax.axis_index("space")
        waits = waits + jnp.minimum(me, 1) + jnp.minimum(lax.axis_size("space") - 1 - me, 1)
    pl.semaphore_wait(barrier, waits)


class Faces:
    def __init__(self, ends, head, tail, low, high, send, recv):
        (self.below, down), (self.above, up) = ends
        self.low, self.high = low, high
        self.down = pltpu.make_async_remote_copy(
            src_ref=head, dst_ref=high, send_sem=send.at[0], recv_sem=recv.at[0],
            device_id=down, device_id_type=pl.DeviceIdType.MESH,
        )
        self.up = pltpu.make_async_remote_copy(
            src_ref=tail, dst_ref=low, send_sem=send.at[1], recv_sem=recv.at[1],
            device_id=up, device_id_type=pl.DeviceIdType.MESH,
        )

    def start(self):
        pl.when(self.below)(self.down.start)
        pl.when(self.above)(self.up.start)

    def finish(self):
        @pl.when(self.below)
        def _():
            self.down.wait_send()
            self.up.wait_recv()

        @pl.when(jnp.logical_not(self.below))
        def _():
            self.low[...] = jnp.zeros(self.low.shape, self.low.dtype)

        @pl.when(self.above)
        def _():
            self.up.wait_send()
            self.down.wait_recv()

        @pl.when(jnp.logical_not(self.above))
        def _():
            self.high[...] = jnp.zeros(self.high.shape, self.high.dtype)


def exchange_body(
    count, slabs, partner_ref, x_ref, mate_ref, low_ref, high_ref, mate_low_ref, mate_high_ref,
    got_a, got_b, stage, send_one, recv_one, send_two, recv_two, send_face, recv_face,
):
    me = lax.axis_index("sample")
    peers = [lax.rem(me + step, count) for step in range(1, count)]
    ends = neighbours(slabs)
    greet([{"sample": peer} for peer in peers], ends)
    got = (got_a, got_b)
    rows = got_a.shape[1]
    layer = low_ref.shape[0]

    def faces(cells, low, high, kind):
        return Faces(
            ends, cells.at[pl.ds(0, layer)], cells.at[pl.ds(count - layer, layer)], low, high,
            send_face.at[kind], recv_face.at[kind],
        )

    def push(src, dst, send, recv, peer):
        return pltpu.make_async_remote_copy(
            src_ref=src, dst_ref=dst, send_sem=send, recv_sem=recv,
            device_id={"sample": peer}, device_id_type=pl.DeviceIdType.MESH,
        )

    first, second = [], []
    for part in range(2):
        span = pl.ds(part * rows, rows)
        first.append([
            push(x_ref.at[peer, span], got[part].at[me], send_one.at[part, place], recv_one.at[part, place], peer)
            for place, peer in enumerate(peers)
        ])
        for copy in first[part]:
            copy.start()
    own = faces(x_ref, low_ref, high_ref, 0)
    own.start()
    for part in range(2):
        span = pl.ds(part * rows, rows)
        got[part][me] = x_ref[me, span]
        for copy in first[part]:
            copy.wait_recv()
        second.append([])
        for place, peer in enumerate(peers):
            stage[part, place] = got[part][partner_ref[peer]]
            copy = push(
                stage.at[part, place], mate_ref.at[me, span],
                send_two.at[part, place], recv_two.at[part, place], peer,
            )
            copy.start()
            second[part].append(copy)
        mate_ref[me, span] = got[part][partner_ref[me]]
    for copies in second:
        for copy in copies:
            copy.wait_recv()
    mates = faces(mate_ref, mate_low_ref, mate_high_ref, 1)
    mates.start()
    for copies in first + second:
        for copy in copies:
            copy.wait_send()
    own.finish()
    mates.finish()


def exchange(x, partner, count, slabs):
    depth, cells, chans = x.shape
    piece = depth * cells // count
    layer = cells // piece
    rows = piece // 2
    dma = pltpu.SemaphoreType.DMA
    vmem = pl.BlockSpec(memory_space=pltpu.VMEM)
    edge = jax.ShapeDtypeStruct((layer, piece, chans), BF16)
    mate, *rest = pl.pallas_call(
        functools.partial(exchange_body, count, slabs),
        out_shape=[jax.ShapeDtypeStruct((count, piece, chans), BF16)] + [edge] * 4,
        in_specs=[pl.BlockSpec(memory_space=pltpu.SMEM), vmem],
        out_specs=[vmem] * 5,
        scratch_shapes=[
            pltpu.VMEM((count, rows, chans), BF16),
            pltpu.VMEM((count, rows, chans), BF16),
            pltpu.VMEM((2, count - 1, rows, chans), BF16),
            dma((2, count - 1)), dma((2, count - 1)), dma((2, count - 1)), dma((2, count - 1)),
            dma((2, 2)), dma((2, 2)),
        ],
        compiler_params=pltpu.CompilerParams(
            collective_id=0, has_side_effects=True, vmem_limit_bytes=VMEM_LIMIT
        ),
    )(partner, x.reshape(count, piece, chans))
    return [mate.reshape(depth, cells, chans)] + [a.reshape(1, cells, chans) for a in rest]


class Total:
    def __init__(self, order, held, landing, full, send, recv):
        self.held, self.landing, self.full, self.send, self.recv = held, landing, full, send, recv
        start, size, base = 0, held.shape[0], 0
        self.plan = []
        for axis, bit in order:
            me = lax.axis_index(axis)
            half = size // 2
            mine = lax.rem(me // (1 << bit), 2)
            peer = {axis: me + (1 - 2 * mine) * (1 << bit)}
            keep = start + mine * half
            self.plan.append((peer, keep, start + (1 - mine) * half, half, base))
            start, size, base = keep, half, base + half
        self.copy = None

    def rows(self, start, size):
        return pl.ds(pl.multiple_of(start, 16), size)

    def begin(self, turn):
        count = len(self.plan)
        if turn < count:
            peer, _, away, half, base = self.plan[turn]
            src = self.held.at[self.rows(away, half)]
            dst = self.landing.at[pl.ds(base, half)]
        else:
            peer, keep, _, half, _ = self.plan[2 * count - 1 - turn]
            if turn == count:
                self.full[self.rows(keep, half)] = self.held[self.rows(keep, half)]
            src = dst = self.full.at[self.rows(keep, half)]
        self.copy = pltpu.make_async_remote_copy(
            src_ref=src, dst_ref=dst, send_sem=self.send.at[turn], recv_sem=self.recv.at[turn],
            device_id=peer, device_id_type=pl.DeviceIdType.MESH,
        )
        self.copy.start()

    def end(self, turn):
        self.copy.wait()
        if turn < len(self.plan):
            _, keep, _, half, base = self.plan[turn]
            span = self.rows(keep, half)
            self.held[span] = (
                self.held[span].astype(F32) + self.landing[pl.ds(base, half)].astype(F32)
            ).astype(BF16)


def sum_orders(count, slabs):
    samples = [("sample", bit) for bit in range(count.bit_length() - 1)]
    spaces = [("space", bit) for bit in range(slabs.bit_length() - 1)]
    return samples[:2] + spaces + samples[2:], samples[:1] + spaces + samples[1:]


def totals_body(count, slabs, one_ref, two_ref, full_one, full_two, held_one, held_two, land_one, land_two, send, recv):
    orders = sum_orders(count, slabs)
    peers = []
    for axis, bit in orders[0]:
        me = lax.axis_index(axis)
        peers.append({axis: me + (1 - 2 * lax.rem(me // (1 << bit), 2)) * (1 << bit)})
    greet(peers, ())
    held_one[...] = one_ref[...]
    held_two[...] = two_ref[...]
    sums = [
        Total(orders[0], held_one, land_one, full_one, send.at[0], recv.at[0]),
        Total(orders[1], held_two, land_two, full_two, send.at[1], recv.at[1]),
    ]
    for turn in range(2 * len(orders[0])):
        for item in sums:
            item.begin(turn)
        for item in sums:
            item.end(turn)


def totals(one, two, count, slabs):
    rows, chans = one.shape
    vmem = pl.BlockSpec(memory_space=pltpu.VMEM)
    buffer = pltpu.VMEM((rows, chans), BF16)
    turns = 2 * len(sum_orders(count, slabs)[0])
    return pl.pallas_call(
        functools.partial(totals_body, count, slabs),
        out_shape=[jax.ShapeDtypeStruct((rows, chans), BF16)] * 2,
        in_specs=[vmem] * 2,
        out_specs=[vmem] * 2,
        scratch_shapes=[buffer] * 4
        + [pltpu.SemaphoreType.DMA((2, turns)), pltpu.SemaphoreType.DMA((2, turns))],
        compiler_params=pltpu.CompilerParams(
            collective_id=1, has_side_effects=True, vmem_limit_bytes=VMEM_LIMIT
        ),
    )(one, two)


def edges(block, width):
    count = lax.axis_size("space")
    low = lax.ppermute(block[-width:], "space", [(i, i + 1) for i in range(count - 1)])
    high = lax.ppermute(block[:width], "space", [(i + 1, i) for i in range(count - 1)])
    return low, high


def shards(volume, first_kernel, second_kernel, partner, coefficient, out_grad):
    _, depth, height, width, chans = volume.shape
    cells = height * width
    me = lax.axis_index("sample")
    own_share = coefficient[me]
    shares = jnp.stack([own_share, 1.0 - own_share])
    x = volume.reshape(depth, cells, chans)
    cot = out_grad.reshape(depth, cells, chans)
    flat_one = first_kernel.reshape(3, 9 * chans, chans)
    flat_two = second_kernel.reshape(3, 9 * chans, chans)
    flipped = jnp.transpose(jnp.flip(second_kernel, (0, 1, 2)), (0, 1, 2, 4, 3)).reshape(
        3, 9 * chans, chans
    )
    count, slabs = lax.axis_size("sample"), lax.axis_size("space")
    mate, low, high, mate_low, mate_high = exchange(x, partner, count, slabs)
    own_pad, mate_pad = (low, x, high), (mate_low, mate, mate_high)
    layer = (depth, cells, chans)
    half = jax.ShapeDtypeStruct(layer, BF16)
    full = jax.ShapeDtypeStruct(layer, F32)
    unit = 2 * depth * cells * 27 * chans * chans
    store_one = pltpu.VMEM((depth + 2, cells + 2 * width, 3 * chans), BF16)
    store_two = pltpu.VMEM((depth + 4, cells + 4 * width, 3 * chans), BF16)
    wide = pltpu.VMEM((4, 9 * chans, 2 * chans), BF16)
    total = pltpu.VMEM((3, 9 * chans, chans), F32)
    hidden, slope_own = call(
        first_kernel_body, width, (shares, *own_pad, flat_one), (half, full), [store_one, wide], unit, 1
    )
    mixed, slope_mate = call(
        mix_body, width, (shares, *mate_pad, flat_one, hidden), (half, full), [store_one, wide], unit, 1
    )
    low, high = edges(mixed, 2)
    result, grad_two = call(
        second_body, width, (low, mixed, high, flat_two, cot), (half, half), [store_two, wide], unit
    )
    terms = jax.ShapeDtypeStruct((3, 9 * chans, chans), BF16)
    second_local = call(
        second_grad_body, width, (low, mixed, high, grad_two), terms, [store_two, total], unit
    )
    low, high = edges(grad_two, 2)
    first_local = call(
        back_body,
        width,
        (low, grad_two, high, flipped, slope_own, slope_mate, *own_pad, *mate_pad),
        terms,
        [store_two, wide, pltpu.VMEM(layer, BF16), pltpu.VMEM(layer, BF16), store_one, total],
        3 * unit,
    )
    shape = first_kernel.shape
    rows = 27 * chans
    unit_rows = 16 * count * slabs
    spare = -rows % unit_rows
    second_sum, first_sum = totals(
        *[jnp.pad(a.reshape(rows, chans), ((0, spare), (0, 0))) for a in (second_local, first_local)],
        count,
        slabs,
    )
    second_sum = second_sum[:rows].astype(F32).reshape(shape)
    first_sum = first_sum[:rows].astype(F32).reshape(shape)
    return result.reshape(volume.shape), first_sum, second_sum


def solution(mesh):
    in_specs = (
        P("sample", "space", None, None, None),
        P(),
        P(),
        P(),
        P(),
        P("sample", "space", None, None, None),
    )
    out_specs = (P("sample", "space", None, None, None), P(), P())
    return jax.shard_map(shards, mesh=mesh, in_specs=in_specs, out_specs=out_specs, check_vma=False)
```

```python
import functools

import jax
import jax.numpy as jnp
from jax import lax
from jax.experimental import pallas as pl
from jax.experimental.pallas import tpu as pltpu
from jax.sharding import PartitionSpec as P

F32 = jnp.float32
BF16 = jnp.bfloat16
VMEM_LIMIT = 56 * 1024 * 1024


def slope(value):
    squash = jax.nn.sigmoid(value)
    return squash * (1.0 + value * (1.0 - squash))


def groups(depth, spread):
    first = [p for p in range(depth) if (p // spread) % 2 == 0]
    return first, [p + spread for p in first]


def frame(store, layer, plane, spread, width):
    cells, chans = plane.shape
    edge = spread * width
    wide = plane.astype(F32)
    column = lax.broadcasted_iota(jnp.int32, plane.shape, 0) % width
    left = jnp.where(column >= spread, pltpu.roll(wide, spread, 0), 0.0).astype(BF16)
    right = jnp.where(column < width - spread, pltpu.roll(wide, cells - spread, 0), 0.0).astype(BF16)
    store[layer, pl.ds(0, edge), :] = jnp.zeros((edge, 3 * chans), BF16)
    store[layer, pl.ds(edge + cells, edge), :] = jnp.zeros((edge, 3 * chans), BF16)
    for place, value in enumerate((left, plane, right)):
        store[layer, pl.ds(edge, cells), pl.ds(place * chans, chans)] = value


def taps(store, layer, spread, width, cells):
    return jnp.concatenate(
        [store[layer, pl.ds(row * spread * width, cells), :] for row in range(3)], axis=1
    )


def fill_pairs(kernel_ref, wide_ref):
    chans = kernel_ref.shape[2]
    for step in range(4):
        for out in range(2):
            depth_tap = step - out
            block = (
                kernel_ref[depth_tap]
                if 0 <= depth_tap < 3
                else jnp.zeros(kernel_ref.shape[1:], BF16)
            )
            wide_ref[step, :, pl.ds(out * chans, chans)] = block


def fill_back(kernel_ref, wide_ref):
    chans = kernel_ref.shape[2]
    for step in range(4):
        for out in range(2):
            depth_tap = step - out
            for place in range(9):
                block = (
                    kernel_ref[2 - depth_tap, pl.ds((8 - place) * chans, chans)]
                    if 0 <= depth_tap < 3
                    else jnp.zeros((chans, chans), BF16)
                )
                wide_ref[step, pl.ds(out * chans, chans), pl.ds(place * chans, chans)] = block


def conv_pairs(store, wide_ref, depth, spread, width, cells, back=False):
    first, _ = groups(depth, spread)
    side = 1 if back else 0
    total = None
    for half in range(2):
        rows = []
        for p in first:
            rows.append(
                jnp.concatenate(
                    [
                        taps(store, p + spread * (2 * half + k), spread, width, cells)
                        for k in range(2)
                    ],
                    axis=1,
                )
            )
        lhs = jnp.concatenate(rows, axis=0)
        rhs = jnp.concatenate([wide_ref[2 * half], wide_ref[2 * half + 1]], axis=side)
        part = lax.dot_general(lhs, rhs, (((1,), (side,)), ((), ())), preferred_element_type=F32)
        total = part if total is None else total + part
    chans = total.shape[1] // 2
    for place, p in enumerate(first):
        for out in range(2):
            yield p + out * spread, total[
                place * cells : (place + 1) * cells, out * chans : (out + 1) * chans
            ]


def grad_blocks(store, grad_at, depth, spread, width, cells):
    ranges = ((0, 2 * spread, (0, 1)), (2 * spread, depth, (0, 1, 2)), (depth, depth + 2 * spread, (1, 2)))
    for low, high, depth_taps in ranges:
        lhs = jnp.concatenate(
            [taps(store, e, spread, width, cells) for e in range(low, high)], axis=0
        )
        columns = []
        for tap in depth_taps:
            layers = []
            for e in range(low, high):
                p = e - spread * tap
                layers.append(grad_at(p if 0 <= p < depth else None))
            columns.append(jnp.concatenate(layers, axis=0))
        rhs = jnp.concatenate(columns, axis=1)
        part = lax.dot_general(lhs, rhs, (((0,), (0,)), ((), ())), preferred_element_type=F32)
        chans = columns[0].shape[1]
        for place, tap in enumerate(depth_taps):
            yield tap, part[:, place * chans : (place + 1) * chans]


def frame_all(store, low_ref, x_ref, high_ref, spread, width, layers=None):
    depth = x_ref.shape[0]
    for layer in range(depth + 2 * spread) if layers is None else layers:
        if layer < spread:
            plane = low_ref[layer]
        elif layer < depth + spread:
            plane = x_ref[layer - spread]
        else:
            plane = high_ref[layer - depth - spread]
        frame(store, layer, plane, spread, width)


def second_body(width, low_ref, mixed_ref, high_ref, kernel_ref, cot_ref, result_ref, grad_ref, store, wide_ref):
    depth, cells, _ = result_ref.shape
    frame_all(store, low_ref, mixed_ref, high_ref, 2, width)
    fill_pairs(kernel_ref, wide_ref)
    for p, value in conv_pairs(store, wide_ref, depth, 2, width, cells):
        squash = jax.nn.sigmoid(value)
        result_ref[p] = (value * squash).astype(BF16)
        grad_ref[p] = (
            cot_ref[p].astype(F32) * (squash * (1.0 + value * (1.0 - squash)))
        ).astype(BF16)


def call(body, width, args, outs, scratch, flops, smem=0):
    vmem = pl.BlockSpec(memory_space=pltpu.VMEM)
    scalar = pl.BlockSpec(memory_space=pltpu.SMEM)
    size = sum(a.size * a.dtype.itemsize for a in args)
    return pl.pallas_call(
        functools.partial(body, width),
        out_shape=outs,
        in_specs=[scalar] * smem + [vmem] * (len(args) - smem),
        out_specs=jax.tree.map(lambda _: vmem, outs),
        scratch_shapes=scratch,
        compiler_params=pltpu.CompilerParams(vmem_limit_bytes=VMEM_LIMIT),
        cost_estimate=pl.CostEstimate(flops=flops, bytes_accessed=size, transcendentals=0),
    )(*args)


def neighbours(count):
    me = lax.axis_index("space")
    return (me > 0, {"space": me - 1}), (me < count - 1, {"space": me + 1})


def greet(peers, ends):
    barrier = pltpu.get_barrier_semaphore()
    for peer in peers:
        pl.semaphore_signal(barrier, inc=1, device_id=peer, device_id_type=pl.DeviceIdType.MESH)
    for exists, peer in ends:

        @pl.when(exists)
        def _(peer=peer):
            pl.semaphore_signal(barrier, inc=1, device_id=peer, device_id_type=pl.DeviceIdType.MESH)

    waits = len(peers)
    if ends:
        me = lax.axis_index("space")
        waits = waits + jnp.minimum(me, 1) + jnp.minimum(lax.axis_size("space") - 1 - me, 1)
    pl.semaphore_wait(barrier, waits)


class Faces:
    def __init__(self, ends, head, tail, low, high, send, recv):
        (self.below, down), (self.above, up) = ends
        self.low, self.high = low, high
        self.down = pltpu.make_async_remote_copy(
            src_ref=head, dst_ref=high, send_sem=send.at[0], recv_sem=recv.at[0],
            device_id=down, device_id_type=pl.DeviceIdType.MESH,
        )
        self.up = pltpu.make_async_remote_copy(
            src_ref=tail, dst_ref=low, send_sem=send.at[1], recv_sem=recv.at[1],
            device_id=up, device_id_type=pl.DeviceIdType.MESH,
        )

    def start(self):
        pl.when(self.below)(self.down.start)
        pl.when(self.above)(self.up.start)

    def finish(self):
        @pl.when(self.below)
        def _():
            self.down.wait_send()
            self.up.wait_recv()

        @pl.when(jnp.logical_not(self.below))
        def _():
            self.low[...] = jnp.zeros(self.low.shape, self.low.dtype)

        @pl.when(self.above)
        def _():
            self.up.wait_send()
            self.down.wait_recv()

        @pl.when(jnp.logical_not(self.above))
        def _():
            self.high[...] = jnp.zeros(self.high.shape, self.high.dtype)


class Total:
    def __init__(self, order, start, size, held, landing, full, send, recv):
        self.held, self.landing, self.full, self.send, self.recv = held, landing, full, send, recv
        base = start
        self.plan = []
        for axis, bit in order:
            me = lax.axis_index(axis)
            half = size // 2
            mine = lax.rem(me // (1 << bit), 2)
            peer = {axis: me + (1 - 2 * mine) * (1 << bit)}
            keep = start + mine * half
            self.plan.append((peer, keep, start + (1 - mine) * half, half, base))
            start, size, base = keep, half, base + half
        self.copy, self.turn = None, -1

    def rows(self, start, size):
        return pl.ds(pl.multiple_of(start, 16), size)

    def run(self, turns):
        for _ in range(turns):
            if self.turn == 2 * len(self.plan):
                return
            if self.turn >= 0:
                self.end(self.turn)
            self.turn += 1
            if self.turn == 2 * len(self.plan):
                return
            self.begin(self.turn)

    def begin(self, turn):
        count = len(self.plan)
        if turn < count:
            peer, _, away, half, base = self.plan[turn]
            src = self.held.at[self.rows(away, half)]
            dst = self.landing.at[pl.ds(base, half)]
        else:
            peer, keep, _, half, _ = self.plan[2 * count - 1 - turn]
            if turn == count:
                self.full[self.rows(keep, half)] = self.held[self.rows(keep, half)]
            src = dst = self.full.at[self.rows(keep, half)]
        self.copy = pltpu.make_async_remote_copy(
            src_ref=src, dst_ref=dst, send_sem=self.send.at[turn], recv_sem=self.recv.at[turn],
            device_id=peer, device_id_type=pl.DeviceIdType.MESH,
        )
        self.copy.start()

    def end(self, turn):
        self.copy.wait()
        if turn < len(self.plan):
            _, keep, _, half, base = self.plan[turn]
            span = self.rows(keep, half)
            self.held[span] = (
                self.held[span].astype(F32) + self.landing[pl.ds(base, half)].astype(F32)
            ).astype(BF16)


def sum_orders(count, slabs):
    samples = [("sample", bit) for bit in range(count.bit_length() - 1)]
    spaces = [("space", bit) for bit in range(slabs.bit_length() - 1)]
    return samples[:2] + spaces + samples[2:], samples[:1] + spaces + samples[1:]


def mixed_body(
    count, slabs, width, partner_ref, share_ref, x_ref, kernel_ref,
    mate_ref, own_low, own_high, mate_low, mate_high, mixed_ref, low_ref, high_ref, slope_own_ref, slope_mate_ref,
    got_a, got_b, stage, hidden, store, wide_ref, send_one, recv_one, send_two, recv_two, send_face, recv_face,
):
    depth, cells, chans = x_ref.shape
    me = lax.axis_index("sample")
    peers = [lax.rem(me + step, count) for step in range(1, count)]
    ends = neighbours(slabs)
    greet([{"sample": peer} for peer in peers], ends)
    got = (got_a, got_b)
    piece = depth * cells // count
    per_layer = cells // piece
    rows = piece // 2

    def span(index, part):
        return index // per_layer, pl.ds(pl.multiple_of(lax.rem(index, per_layer) * piece + part * rows, 16), rows)

    def push(src, dst, send, recv, peer):
        return pltpu.make_async_remote_copy(
            src_ref=src, dst_ref=dst, send_sem=send, recv_sem=recv,
            device_id={"sample": peer}, device_id_type=pl.DeviceIdType.MESH,
        )

    def faces(block, edge, low, high, kind):
        return Faces(
            ends, block.at[pl.ds(0, edge)], block.at[pl.ds(depth - edge, edge)], low, high,
            send_face.at[kind], recv_face.at[kind],
        )

    first, second = [], []
    for part in range(2):
        first.append([
            push(x_ref.at[span(peer, part)], got[part].at[me], send_one.at[part, place], recv_one.at[part, place], peer)
            for place, peer in enumerate(peers)
        ])
        for copy in first[part]:
            copy.start()
        if part == 0:
            own = faces(x_ref, 1, own_low, own_high, 0)
            own.start()
    share = share_ref[me]
    fill_pairs(kernel_ref, wide_ref)
    frame_all(store, None, x_ref, None, 1, width, range(1, depth + 1))
    own.finish()
    frame_all(store, own_low, x_ref, own_high, 1, width, (0, depth + 1))
    for p, value in conv_pairs(store, wide_ref, depth, 1, width, cells):
        squash = jax.nn.sigmoid(value)
        hidden[p] = (value * squash).astype(BF16)
        slope_own_ref[p] = share * (squash * (1.0 + value * (1.0 - squash)))
    for part in range(2):
        got[part][me] = x_ref[span(me, part)]
        for copy in first[part]:
            copy.wait_recv()
        second.append([])
        for place, peer in enumerate(peers):
            stage[part, place] = got[part][partner_ref[peer]]
            copy = push(
                stage.at[part, place], mate_ref.at[span(me, part)],
                send_two.at[part, place], recv_two.at[part, place], peer,
            )
            copy.start()
            second[part].append(copy)
        mate_ref[span(me, part)] = got[part][partner_ref[me]]
    for copies in second:
        for copy in copies:
            copy.wait_recv()
    mates = faces(mate_ref, 1, mate_low, mate_high, 1)
    mates.start()
    frame_all(store, None, mate_ref, None, 1, width, range(1, depth + 1))
    mates.finish()
    frame_all(store, mate_low, mate_ref, mate_high, 1, width, (0, depth + 1))
    for p, value in conv_pairs(store, wide_ref, depth, 1, width, cells):
        squash = jax.nn.sigmoid(value)
        other = (value * squash).astype(BF16).astype(F32)
        mixed_ref[p] = (share * hidden[p].astype(F32) + (1.0 - share) * other).astype(BF16)
        slope_mate_ref[p] = (1.0 - share) * (squash * (1.0 + value * (1.0 - squash)))
    mixes = faces(mixed_ref, 2, low_ref, high_ref, 2)
    mixes.start()
    for copies in first + second:
        for copy in copies:
            copy.wait_send()
    mixes.finish()


def mixed_call(x, kernel, partner, coefficient, count, slabs, width):
    depth, cells, chans = x.shape
    rows = depth * cells // count // 2
    dma = pltpu.SemaphoreType.DMA
    vmem = pl.BlockSpec(memory_space=pltpu.VMEM)
    smem = pl.BlockSpec(memory_space=pltpu.SMEM)

    def layers(n, dtype=BF16):
        return jax.ShapeDtypeStruct((n, cells, chans), dtype)

    return pl.pallas_call(
        functools.partial(mixed_body, count, slabs, width),
        out_shape=[layers(depth)] + [layers(1)] * 4 + [layers(depth), layers(2), layers(2)] + [layers(depth, F32)] * 2,
        in_specs=[smem, smem, vmem, vmem],
        out_specs=[vmem] * 10,
        scratch_shapes=[
            pltpu.VMEM((count, rows, chans), BF16),
            pltpu.VMEM((count, rows, chans), BF16),
            pltpu.VMEM((2, count - 1, rows, chans), BF16),
            pltpu.VMEM((depth, cells, chans), BF16),
            pltpu.VMEM((depth + 2, cells + 2 * width, 3 * chans), BF16),
            pltpu.VMEM((4, 9 * chans, 2 * chans), BF16),
            dma((2, count - 1)), dma((2, count - 1)), dma((2, count - 1)), dma((2, count - 1)),
            dma((3, 2)), dma((3, 2)),
        ],
        compiler_params=pltpu.CompilerParams(
            collective_id=0, has_side_effects=True, vmem_limit_bytes=VMEM_LIMIT
        ),
    )(partner, coefficient, x, kernel)


def grads_body(
    count, slabs, width, low_ref, mixed_ref, high_ref, grad_ref, kernel_ref, slope_own_ref, slope_mate_ref,
    own_low, own_ref, own_high, mate_low, mate_ref, mate_high, out_one, out_two,
    grad_low, grad_high, store_two, store_one, wide_ref, term_own, term_mate, total,
    held_one, held_two, land_one, land_two, full_one, full_two, send, recv, send_face, recv_face,
):
    depth, cells, chans = grad_ref.shape
    orders = sum_orders(count, slabs)
    peers = []
    for axis, bit in orders[0]:
        me = lax.axis_index(axis)
        peers.append({axis: me + (1 - 2 * lax.rem(me // (1 << bit), 2)) * (1 << bit)})
    ends = neighbours(slabs)
    greet(peers, ends)
    size = held_one.shape[0]
    used = 27 * chans
    unit = 16 * count * slabs
    cut = (size // unit + 1) // 2 * unit

    def lanes(kind, held, land, full):
        made = []
        for lane, (start, end) in enumerate(((0, cut), (cut, size))):
            if end > start:
                made.append(
                    Total(orders[lane], start, end - start, held, land, full, send.at[kind, lane], recv.at[kind, lane])
                )
        return made

    def advance(made, turns=1):
        for _ in range(turns):
            for lane in made:
                lane.run(1)

    def hand_over(held):
        for tap in range(3):
            held[pl.ds(tap * 9 * chans, 9 * chans)] = total[tap].astype(BF16)
        if size > used:
            held[pl.ds(used, size - used)] = jnp.zeros((size - used, chans), BF16)

    faces = Faces(
        ends, grad_ref.at[pl.ds(0, 2)], grad_ref.at[pl.ds(depth - 2, 2)], grad_low, grad_high, send_face, recv_face
    )
    faces.start()

    def grad_at(ref, p):
        return jnp.zeros((cells, chans), BF16) if p is None else ref[p]

    frame_all(store_two, low_ref, mixed_ref, high_ref, 2, width)
    total[...] = jnp.zeros_like(total)
    for tap, part in grad_blocks(store_two, functools.partial(grad_at, grad_ref), depth, 2, width, cells):
        total[tap] += part
    hand_over(held_two)
    seconds = lanes(1, held_two, land_two, full_two)
    advance(seconds)
    fill_back(kernel_ref, wide_ref)
    frame_all(store_two, None, grad_ref, None, 2, width, range(2, depth + 2))
    faces.finish()
    frame_all(store_two, grad_low, grad_ref, grad_high, 2, width, (0, 1, depth + 2, depth + 3))
    advance(seconds)
    for p, value in conv_pairs(store_two, wide_ref, depth, 2, width, cells, back=True):
        value = value.astype(BF16).astype(F32)
        term_own[p] = (value * slope_own_ref[p]).astype(BF16)
        term_mate[p] = (value * slope_mate_ref[p]).astype(BF16)
    advance(seconds)
    total[...] = jnp.zeros_like(total)
    for slab, term in (((own_low, own_ref, own_high), term_own), ((mate_low, mate_ref, mate_high), term_mate)):
        frame_all(store_one, *slab, 1, width)
        advance(seconds)
        for tap, part in grad_blocks(store_one, functools.partial(grad_at, term), depth, 1, width, cells):
            total[tap] += part
            if tap == 2:
                advance(seconds)
    hand_over(held_one)
    firsts = lanes(0, held_one, land_one, full_one)
    for _ in range(2 * len(orders[0]) + 1):
        advance(firsts)
        advance(seconds)
    out_one[...] = full_one[pl.ds(0, used)]
    out_two[...] = full_two[pl.ds(0, used)]


def grads_call(args, count, slabs, width):
    depth, cells, chans = args[3].shape
    used = 27 * chans
    size = used + -used % (16 * count * slabs)
    turns = 2 * len(sum_orders(count, slabs)[0])
    vmem = pl.BlockSpec(memory_space=pltpu.VMEM)
    dma = pltpu.SemaphoreType.DMA
    buffer = pltpu.VMEM((size, chans), BF16)
    return pl.pallas_call(
        functools.partial(grads_body, count, slabs, width),
        out_shape=[jax.ShapeDtypeStruct((used, chans), BF16)] * 2,
        in_specs=[vmem] * len(args),
        out_specs=[vmem] * 2,
        scratch_shapes=[
            pltpu.VMEM((2, cells, chans), BF16),
            pltpu.VMEM((2, cells, chans), BF16),
            pltpu.VMEM((depth + 4, cells + 4 * width, 3 * chans), BF16),
            pltpu.VMEM((depth + 2, cells + 2 * width, 3 * chans), BF16),
            pltpu.VMEM((4, 2 * chans, 9 * chans), BF16),
            pltpu.VMEM((depth, cells, chans), BF16),
            pltpu.VMEM((depth, cells, chans), BF16),
            pltpu.VMEM((3, 9 * chans, chans), F32),
        ]
        + [buffer] * 6
        + [dma((2, 2, turns)), dma((2, 2, turns)), dma((2,)), dma((2,))],
        compiler_params=pltpu.CompilerParams(
            collective_id=1, has_side_effects=True, vmem_limit_bytes=VMEM_LIMIT
        ),
    )(*args)


def shards(volume, first_kernel, second_kernel, partner, coefficient, out_grad):
    _, depth, height, width, chans = volume.shape
    cells = height * width
    count, slabs = lax.axis_size("sample"), lax.axis_size("space")
    x = volume.reshape(depth, cells, chans)
    cot = out_grad.reshape(depth, cells, chans)
    flat_one = first_kernel.reshape(3, 9 * chans, chans)
    flat_two = second_kernel.reshape(3, 9 * chans, chans)
    mate, own_low, own_high, mate_low, mate_high, mixed, low, high, slope_own, slope_mate = mixed_call(
        x, flat_one, partner, coefficient, count, slabs, width
    )
    half = jax.ShapeDtypeStruct((depth, cells, chans), BF16)
    result, grad_two = call(
        second_body,
        width,
        (low, mixed, high, flat_two, cot),
        (half, half),
        [
            pltpu.VMEM((depth + 4, cells + 4 * width, 3 * chans), BF16),
            pltpu.VMEM((4, 9 * chans, 2 * chans), BF16),
        ],
        2 * depth * cells * 27 * chans * chans,
    )
    first_sum, second_sum = grads_call(
        (low, mixed, high, grad_two, flat_two, slope_own, slope_mate, own_low, x, own_high, mate_low, mate, mate_high),
        count,
        slabs,
        width,
    )
    shape = first_kernel.shape
    return (
        result.reshape(volume.shape),
        first_sum.astype(F32).reshape(shape),
        second_sum.astype(F32).reshape(shape),
    )


def solution(mesh):
    in_specs = (
        P("sample", "space", None, None, None),
        P(),
        P(),
        P(),
        P(),
        P("sample", "space", None, None, None),
    )
    out_specs = (P("sample", "space", None, None, None), P(), P())
    return jax.shard_map(shards, mesh=mesh, in_specs=in_specs, out_specs=out_specs, check_vma=False)
```

```python
import functools

import jax
import jax.numpy as jnp
from jax import lax
from jax.experimental import pallas as pl
from jax.experimental.pallas import tpu as pltpu
from jax.sharding import PartitionSpec as P

F32 = jnp.float32
BF16 = jnp.bfloat16
VMEM_LIMIT = 56 * 1024 * 1024


def slope(value):
    squash = jax.nn.sigmoid(value)
    return squash * (1.0 + value * (1.0 - squash))


def groups(depth, spread):
    return [p for p in range(depth) if (p // spread) % 2 == 0]


def frame(store, layer, plane, spread, width):
    cells, chans = plane.shape
    edge = spread * width
    wide = plane.astype(F32)
    column = lax.broadcasted_iota(jnp.int32, plane.shape, 0) % width
    left = jnp.where(column >= spread, pltpu.roll(wide, spread, 0), 0.0).astype(BF16)
    right = jnp.where(column < width - spread, pltpu.roll(wide, cells - spread, 0), 0.0).astype(BF16)
    store[layer, pl.ds(0, edge), :] = jnp.zeros((edge, 3 * chans), BF16)
    store[layer, pl.ds(edge + cells, edge), :] = jnp.zeros((edge, 3 * chans), BF16)
    for place, value in enumerate((left, plane, right)):
        store[layer, pl.ds(edge, cells), pl.ds(place * chans, chans)] = value


def taps(store, layer, spread, width, cells):
    return jnp.concatenate(
        [store[layer, pl.ds(row * spread * width, cells), :] for row in range(3)], axis=1
    )


def fill_pairs(kernel_ref, wide_ref):
    chans = kernel_ref.shape[2]
    for step in range(4):
        for out in range(2):
            depth_tap = step - out
            block = (
                kernel_ref[depth_tap]
                if 0 <= depth_tap < 3
                else jnp.zeros(kernel_ref.shape[1:], BF16)
            )
            wide_ref[step, :, pl.ds(out * chans, chans)] = block


def fill_back(kernel_ref, wide_ref):
    chans = kernel_ref.shape[2]
    for step in range(4):
        for out in range(2):
            depth_tap = step - out
            for place in range(9):
                block = (
                    kernel_ref[2 - depth_tap, pl.ds((8 - place) * chans, chans)]
                    if 0 <= depth_tap < 3
                    else jnp.zeros((chans, chans), BF16)
                )
                wide_ref[step, pl.ds(out * chans, chans), pl.ds(place * chans, chans)] = block


def conv_pairs(store, wide_ref, first, spread, width, cells, back=False):
    side = 1 if back else 0
    total = None
    for half in range(2):
        rows = []
        for p in first:
            rows.append(
                jnp.concatenate(
                    [
                        taps(store, p + spread * (2 * half + k), spread, width, cells)
                        for k in range(2)
                    ],
                    axis=1,
                )
            )
        lhs = jnp.concatenate(rows, axis=0)
        rhs = jnp.concatenate([wide_ref[2 * half], wide_ref[2 * half + 1]], axis=side)
        part = lax.dot_general(lhs, rhs, (((1,), (side,)), ((), ())), preferred_element_type=F32)
        total = part if total is None else total + part
    chans = total.shape[1] // 2
    for place, p in enumerate(first):
        for out in range(2):
            yield p + out * spread, total[
                place * cells : (place + 1) * cells, out * chans : (out + 1) * chans
            ]


def grad_blocks(store, grad_at, depth, spread, width, cells):
    ranges = ((0, 2 * spread, (0, 1)), (2 * spread, depth, (0, 1, 2)), (depth, depth + 2 * spread, (1, 2)))
    for low, high, depth_taps in ranges:
        lhs = jnp.concatenate(
            [taps(store, e, spread, width, cells) for e in range(low, high)], axis=0
        )
        columns = []
        for tap in depth_taps:
            layers = []
            for e in range(low, high):
                p = e - spread * tap
                layers.append(grad_at(p if 0 <= p < depth else None))
            columns.append(jnp.concatenate(layers, axis=0))
        rhs = jnp.concatenate(columns, axis=1)
        part = lax.dot_general(lhs, rhs, (((0,), (0,)), ((), ())), preferred_element_type=F32)
        chans = columns[0].shape[1]
        for place, tap in enumerate(depth_taps):
            yield tap, part[:, place * chans : (place + 1) * chans]


def frame_all(store, low_ref, x_ref, high_ref, spread, width, layers=None):
    depth = x_ref.shape[0]
    for layer in range(depth + 2 * spread) if layers is None else layers:
        if layer < spread:
            plane = low_ref[layer]
        elif layer < depth + spread:
            plane = x_ref[layer - spread]
        else:
            plane = high_ref[layer - depth - spread]
        frame(store, layer, plane, spread, width)


def neighbours(count):
    me = lax.axis_index("space")
    return (me > 0, {"space": me - 1}), (me < count - 1, {"space": me + 1})


def greet(peers, ends):
    barrier = pltpu.get_barrier_semaphore()
    for peer in peers:
        pl.semaphore_signal(barrier, inc=1, device_id=peer, device_id_type=pl.DeviceIdType.MESH)
    for exists, peer in ends:

        @pl.when(exists)
        def _(peer=peer):
            pl.semaphore_signal(barrier, inc=1, device_id=peer, device_id_type=pl.DeviceIdType.MESH)

    waits = len(peers)
    if ends:
        me = lax.axis_index("space")
        waits = waits + jnp.minimum(me, 1) + jnp.minimum(lax.axis_size("space") - 1 - me, 1)
    pl.semaphore_wait(barrier, waits)


class Faces:
    def __init__(self, ends, head, tail, low, high, send, recv):
        (self.below, down), (self.above, up) = ends
        self.low, self.high = low, high
        self.down = pltpu.make_async_remote_copy(
            src_ref=head, dst_ref=high, send_sem=send.at[0], recv_sem=recv.at[0],
            device_id=down, device_id_type=pl.DeviceIdType.MESH,
        )
        self.up = pltpu.make_async_remote_copy(
            src_ref=tail, dst_ref=low, send_sem=send.at[1], recv_sem=recv.at[1],
            device_id=up, device_id_type=pl.DeviceIdType.MESH,
        )

    def start(self):
        pl.when(self.below)(self.down.start)
        pl.when(self.above)(self.up.start)

    def finish(self):
        @pl.when(self.below)
        def _():
            self.down.wait_send()
            self.up.wait_recv()

        @pl.when(jnp.logical_not(self.below))
        def _():
            self.low[...] = jnp.zeros(self.low.shape, self.low.dtype)

        @pl.when(self.above)
        def _():
            self.up.wait_send()
            self.down.wait_recv()

        @pl.when(jnp.logical_not(self.above))
        def _():
            self.high[...] = jnp.zeros(self.high.shape, self.high.dtype)


class Total:
    def __init__(self, order, start, size, held, landing, full, send, recv):
        self.held, self.landing, self.full, self.send, self.recv = held, landing, full, send, recv
        base = start
        self.plan = []
        for axis, low, members in order:
            me = lax.axis_index(axis)
            place = lax.rem(me // low, members)
            part = size // members
            others = []
            for step in range(1, members):
                other = lax.rem(place + step, members)
                others.append(({axis: me + (other - place) * low}, start + other * part, base))
                base += part
            start, size = start + place * part, part
            self.plan.append((others, start, part))
        self.copies, self.turn = [], -1

    def rows(self, start, size):
        return pl.ds(pl.multiple_of(start, 16), size)

    def advance(self):
        if self.turn == 2 * len(self.plan):
            return
        if self.turn >= 0:
            self.end(self.turn)
        self.turn += 1
        if self.turn < 2 * len(self.plan):
            self.begin(self.turn)

    def begin(self, turn):
        count = len(self.plan)
        scatter = turn < count
        others, keep, part = self.plan[turn if scatter else 2 * count - 1 - turn]
        if turn == count:
            self.full[self.rows(keep, part)] = self.held[self.rows(keep, part)]
        self.copies = []
        for place, (peer, away, base) in enumerate(others):
            if scatter:
                src, dst = self.held.at[self.rows(away, part)], self.landing.at[pl.ds(base, part)]
            else:
                src = dst = self.full.at[self.rows(keep, part)]
            copy = pltpu.make_async_remote_copy(
                src_ref=src, dst_ref=dst, send_sem=self.send.at[turn, place], recv_sem=self.recv.at[turn, place],
                device_id=peer, device_id_type=pl.DeviceIdType.MESH,
            )
            copy.start()
            self.copies.append(copy)

    def end(self, turn):
        for copy in self.copies:
            copy.wait()
        if turn < len(self.plan):
            others, keep, part = self.plan[turn]
            span = self.rows(keep, part)
            value = self.held[span].astype(F32)
            for _, _, base in others:
                value = value + self.landing[pl.ds(base, part)].astype(F32)
            self.held[span] = value.astype(BF16)


def stages(axis, first, last):
    made = []
    while first < last:
        bits = min(2, last - first)
        made.append((axis, 1 << first, 1 << bits))
        first += bits
    return made


def sum_orders(count, slabs):
    bits = count.bit_length() - 1
    core = stages("sample", 0, min(1, bits))
    near = stages("sample", min(1, bits), min(2, bits))
    far = stages("sample", min(2, bits), bits)
    spaces = stages("space", 0, slabs.bit_length() - 1)
    return core + near + spaces + far, core + spaces + near + far


def whole_body(
    count, slabs, width, partner_ref, share_ref, x_ref, kernel_one_ref, kernel_two_ref, cot_ref,
    result_ref, out_one, out_two,
    got_a, got_b, stage, hidden, mate_ref, faces_one, faces_two, mixed_ref, grad_ref, slope_own_ref, slope_mate_ref,
    store_own, store_mate, store_mix, store_grad, wide_one, wide_two, wide_back, term_own, term_mate, total,
    held_one, held_two, land_one, land_two, full_one, full_two,
    send_one, recv_one, send_two, recv_two, send_face, recv_face, send, recv,
):
    depth, cells, chans = x_ref.shape
    me = lax.axis_index("sample")
    peers = [lax.rem(me + step, count) for step in range(1, count)]
    ends = neighbours(slabs)
    orders = sum_orders(count, slabs)
    far = []
    for axis, low, members in orders[0]:
        if axis == "space":
            at = lax.axis_index(axis)
            place = lax.rem(at // low, members)
            far += [{axis: at + (lax.rem(place + step, members) - place) * low} for step in range(1, members)]
    greet([{"sample": peer} for peer in peers] + far, ends)
    got = (got_a, got_b)
    piece = depth * cells // count
    per_layer = cells // piece
    rows = piece // 2

    def span(index, part):
        return index // per_layer, pl.ds(pl.multiple_of(lax.rem(index, per_layer) * piece + part * rows, 16), rows)

    def push(src, dst, send, recv, peer):
        return pltpu.make_async_remote_copy(
            src_ref=src, dst_ref=dst, send_sem=send, recv_sem=recv,
            device_id={"sample": peer}, device_id_type=pl.DeviceIdType.MESH,
        )

    def faces(block, edge, low, high, kind):
        return Faces(
            ends, block.at[pl.ds(0, edge)], block.at[pl.ds(depth - edge, edge)], low, high,
            send_face.at[kind], recv_face.at[kind],
        )

    own_low, own_high, mate_low, mate_high = [faces_one.at[pl.ds(k, 1)] for k in range(4)]
    mix_low, mix_high, grad_low, grad_high = [faces_two.at[pl.ds(2 * k, 2)] for k in range(4)]

    first, second = [], []
    for part in range(2):
        first.append([
            push(x_ref.at[span(peer, part)], got[part].at[me], send_one.at[part, place], recv_one.at[part, place], peer)
            for place, peer in enumerate(peers)
        ])
        for copy in first[part]:
            copy.start()
        if part == 0:
            own = faces(x_ref, 1, own_low, own_high, 0)
            own.start()
    share = share_ref[me]
    fill_pairs(kernel_one_ref, wide_one)
    frame_all(store_own, None, x_ref, None, 1, width, range(1, depth + 1))
    for part in range(2):
        got[part][me] = x_ref[span(me, part)]
        for copy in first[part]:
            copy.wait_recv()
        second.append([])
        for place, peer in enumerate(peers):
            stage[part, place] = got[part][partner_ref[peer]]
            copy = push(
                stage.at[part, place], mate_ref.at[span(me, part)],
                send_two.at[part, place], recv_two.at[part, place], peer,
            )
            copy.start()
            second[part].append(copy)
        mate_ref[span(me, part)] = got[part][partner_ref[me]]

    own.finish()
    frame_all(store_own, own_low, x_ref, own_high, 1, width, (0, depth + 1))
    for p, value in conv_pairs(store_own, wide_one, groups(depth, 1), 1, width, cells):
        squash = jax.nn.sigmoid(value)
        hidden[p] = (value * squash).astype(BF16)
        slope_own_ref[p] = share * (squash * (1.0 + value * (1.0 - squash)))
    fill_pairs(kernel_two_ref, wide_two)
    fill_back(kernel_two_ref, wide_back)
    for copies in second:
        for copy in copies:
            copy.wait_recv()
    mates = faces(mate_ref, 1, mate_low, mate_high, 1)
    mates.start()
    frame_all(store_mate, None, mate_ref, None, 1, width, range(1, depth + 1))
    mates.finish()
    frame_all(store_mate, mate_low, mate_ref, mate_high, 1, width, (0, depth + 1))

    def mix(pairs):
        for p, value in conv_pairs(store_mate, wide_one, pairs, 1, width, cells):
            squash = jax.nn.sigmoid(value)
            other = (value * squash).astype(BF16).astype(F32)
            mixed_ref[p] = (share * hidden[p].astype(F32) + (1.0 - share) * other).astype(BF16)
            slope_mate_ref[p] = (1.0 - share) * (squash * (1.0 + value * (1.0 - squash)))

    pairs = groups(depth, 1)
    mix([pairs[0], pairs[-1]])
    mixes = faces(mixed_ref, 2, mix_low, mix_high, 2)
    mixes.start()
    mix(pairs[1:-1])
    frame_all(store_mix, None, mixed_ref, None, 2, width, range(2, depth + 2))
    for copies in first + second:
        for copy in copies:
            copy.wait_send()
    mixes.finish()
    frame_all(store_mix, mix_low, mixed_ref, mix_high, 2, width, (0, 1, depth + 2, depth + 3))

    for p, value in conv_pairs(store_mix, wide_two, groups(depth, 2), 2, width, cells):
        squash = jax.nn.sigmoid(value)
        result_ref[p] = (value * squash).astype(BF16)
        grad_ref[p] = (cot_ref[p].astype(F32) * (squash * (1.0 + value * (1.0 - squash)))).astype(BF16)
    backs = faces(grad_ref, 2, grad_low, grad_high, 3)
    backs.start()

    size = held_one.shape[0]
    used = 27 * chans
    unit = 16 * count * slabs
    cut = (size // unit + 1) // 2 * unit

    def lanes(kind, held, land, full):
        made = []
        for lane, (start, end) in enumerate(((0, cut), (cut, size))):
            if end > start:
                made.append(
                    Total(orders[lane], start, end - start, held, land, full, send.at[kind, lane], recv.at[kind, lane])
                )
        return made

    def advance(made):
        for lane in made:
            lane.advance()

    def hand_over(held):
        for tap in range(3):
            held[pl.ds(tap * 9 * chans, 9 * chans)] = total[tap].astype(BF16)
        if size > used:
            held[pl.ds(used, size - used)] = jnp.zeros((size - used, chans), BF16)

    def grad_at(ref, p):
        return jnp.zeros((cells, chans), BF16) if p is None else ref[p]

    total[...] = jnp.zeros_like(total)
    for tap, part in grad_blocks(store_mix, functools.partial(grad_at, grad_ref), depth, 2, width, cells):
        total[tap] += part
    hand_over(held_two)
    seconds = lanes(1, held_two, land_two, full_two)
    advance(seconds)
    frame_all(store_grad, None, grad_ref, None, 2, width, range(2, depth + 2))
    backs.finish()
    frame_all(store_grad, grad_low, grad_ref, grad_high, 2, width, (0, 1, depth + 2, depth + 3))
    for p, value in conv_pairs(store_grad, wide_back, groups(depth, 2), 2, width, cells, back=True):
        value = value.astype(BF16).astype(F32)
        term_own[p] = (value * slope_own_ref[p]).astype(BF16)
        term_mate[p] = (value * slope_mate_ref[p]).astype(BF16)
    advance(seconds)
    total[...] = jnp.zeros_like(total)
    for store, term in ((store_own, term_own), (store_mate, term_mate)):
        for tap, part in grad_blocks(store, functools.partial(grad_at, term), depth, 1, width, cells):
            total[tap] += part
        advance(seconds)
    hand_over(held_one)
    firsts = lanes(0, held_one, land_one, full_one)
    for _ in range(2 * len(orders[0]) + 1):
        advance(firsts)
        advance(seconds)
    out_one[...] = full_one[pl.ds(0, used)]
    out_two[...] = full_two[pl.ds(0, used)]


def whole_call(args, count, slabs, width):
    depth, cells, chans = args[2].shape
    rows = depth * cells // count // 2
    used = 27 * chans
    size = used + -used % (16 * count * slabs)
    turns = 2 * len(sum_orders(count, slabs)[0])
    vmem = pl.BlockSpec(memory_space=pltpu.VMEM)
    smem = pl.BlockSpec(memory_space=pltpu.SMEM)
    dma = pltpu.SemaphoreType.DMA
    slab = pltpu.VMEM((depth, cells, chans), BF16)
    wide_slab = pltpu.VMEM((depth, cells, chans), F32)
    sums = jax.ShapeDtypeStruct((used, chans), BF16)
    return pl.pallas_call(
        functools.partial(whole_body, count, slabs, width),
        out_shape=[jax.ShapeDtypeStruct((depth, cells, chans), BF16), sums, sums],
        in_specs=[smem, smem] + [vmem] * 4,
        out_specs=[vmem] * 3,
        scratch_shapes=[
            pltpu.VMEM((count, rows, chans), BF16),
            pltpu.VMEM((count, rows, chans), BF16),
            pltpu.VMEM((2, count - 1, rows, chans), BF16),
            slab,
            slab,
            pltpu.VMEM((4, cells, chans), BF16),
            pltpu.VMEM((8, cells, chans), BF16),
            slab,
            slab,
            wide_slab,
            wide_slab,
            pltpu.VMEM((depth + 2, cells + 2 * width, 3 * chans), BF16),
            pltpu.VMEM((depth + 2, cells + 2 * width, 3 * chans), BF16),
            pltpu.VMEM((depth + 4, cells + 4 * width, 3 * chans), BF16),
            pltpu.VMEM((depth + 4, cells + 4 * width, 3 * chans), BF16),
            pltpu.VMEM((4, 9 * chans, 2 * chans), BF16),
            pltpu.VMEM((4, 9 * chans, 2 * chans), BF16),
            pltpu.VMEM((4, 2 * chans, 9 * chans), BF16),
            slab,
            slab,
            pltpu.VMEM((3, 9 * chans, chans), F32),
        ]
        + [pltpu.VMEM((size, chans), BF16)] * 6
        + [dma((2, count - 1))] * 4
        + [dma((4, 2))] * 2
        + [dma((2, 2, turns, 3))] * 2,
        compiler_params=pltpu.CompilerParams(
            collective_id=0, has_side_effects=True, vmem_limit_bytes=VMEM_LIMIT
        ),
    )(*args)


def shards(volume, first_kernel, second_kernel, partner, coefficient, out_grad):
    _, depth, height, width, chans = volume.shape
    cells = height * width
    count, slabs = lax.axis_size("sample"), lax.axis_size("space")
    result, first_sum, second_sum = whole_call(
        (
            partner,
            coefficient,
            volume.reshape(depth, cells, chans),
            first_kernel.reshape(3, 9 * chans, chans),
            second_kernel.reshape(3, 9 * chans, chans),
            out_grad.reshape(depth, cells, chans),
        ),
        count,
        slabs,
        width,
    )
    shape = first_kernel.shape
    return (
        result.reshape(volume.shape),
        first_sum.astype(F32).reshape(shape),
        second_sum.astype(F32).reshape(shape),
    )


def solution(mesh):
    in_specs = (
        P("sample", "space", None, None, None),
        P(),
        P(),
        P(),
        P(),
        P("sample", "space", None, None, None),
    )
    out_specs = (P("sample", "space", None, None, None), P(), P())
    return jax.shard_map(shards, mesh=mesh, in_specs=in_specs, out_specs=out_specs, check_vma=False)
```

```python
import functools

import jax
import jax.numpy as jnp
from jax import lax
from jax.experimental import pallas as pl
from jax.experimental.pallas import tpu as pltpu
from jax.sharding import PartitionSpec as P

F32 = jnp.float32
BF16 = jnp.bfloat16
VMEM_LIMIT = 56 * 1024 * 1024


def slope(value):
    squash = jax.nn.sigmoid(value)
    return squash * (1.0 + value * (1.0 - squash))


def groups(depth, spread):
    return [p for p in range(depth) if (p // spread) % 2 == 0]


def frame(store, layer, plane, spread, width):
    cells, chans = plane.shape
    edge = spread * width
    wide = plane.astype(F32)
    column = lax.broadcasted_iota(jnp.int32, plane.shape, 0) % width
    left = jnp.where(column >= spread, pltpu.roll(wide, spread, 0), 0.0).astype(BF16)
    right = jnp.where(column < width - spread, pltpu.roll(wide, cells - spread, 0), 0.0).astype(BF16)
    store[layer, pl.ds(0, edge), :] = jnp.zeros((edge, 3 * chans), BF16)
    store[layer, pl.ds(edge + cells, edge), :] = jnp.zeros((edge, 3 * chans), BF16)
    for place, value in enumerate((left, plane, right)):
        store[layer, pl.ds(edge, cells), pl.ds(place * chans, chans)] = value


def taps(store, layer, spread, width, cells):
    return jnp.concatenate(
        [store[layer, pl.ds(row * spread * width, cells), :] for row in range(3)], axis=1
    )


def fill_pairs(kernel_ref, wide_ref):
    chans = kernel_ref.shape[2]
    for step in range(4):
        for out in range(2):
            depth_tap = step - out
            block = (
                kernel_ref[depth_tap]
                if 0 <= depth_tap < 3
                else jnp.zeros(kernel_ref.shape[1:], BF16)
            )
            wide_ref[step, :, pl.ds(out * chans, chans)] = block


def fill_back(kernel_ref, wide_ref):
    chans = kernel_ref.shape[2]
    for step in range(4):
        for out in range(2):
            depth_tap = step - out
            for place in range(9):
                block = (
                    kernel_ref[2 - depth_tap, pl.ds((8 - place) * chans, chans)]
                    if 0 <= depth_tap < 3
                    else jnp.zeros((chans, chans), BF16)
                )
                wide_ref[step, pl.ds(out * chans, chans), pl.ds(place * chans, chans)] = block


def conv_pairs(store, wide_ref, pairs, spread, width, cells, back=False):
    for at in range(0, len(pairs), 2):
        yield from conv_chunk(store, wide_ref, pairs[at : at + 2], spread, width, cells, back)


def conv_chunk(store, wide_ref, first, spread, width, cells, back):
    side = 1 if back else 0
    total = None
    for half in range(2):
        rows = []
        for p in first:
            rows.append(
                jnp.concatenate(
                    [
                        taps(store, p + spread * (2 * half + k), spread, width, cells)
                        for k in range(2)
                    ],
                    axis=1,
                )
            )
        lhs = jnp.concatenate(rows, axis=0)
        rhs = jnp.concatenate([wide_ref[2 * half], wide_ref[2 * half + 1]], axis=side)
        part = lax.dot_general(lhs, rhs, (((1,), (side,)), ((), ())), preferred_element_type=F32)
        total = part if total is None else total + part
    chans = total.shape[1] // 2
    for place, p in enumerate(first):
        for out in range(2):
            yield p + out * spread, total[
                place * cells : (place + 1) * cells, out * chans : (out + 1) * chans
            ]


def grad_blocks(store, grad_at, depth, spread, width, cells):
    ranges = ((2 * spread, depth, (0, 1, 2)), (0, 2 * spread, (0, 1)), (depth, depth + 2 * spread, (1, 2)))
    for low, high, depth_taps in ranges:
        lhs = jnp.concatenate(
            [taps(store, e, spread, width, cells) for e in range(low, high)], axis=0
        )
        columns = []
        for tap in depth_taps:
            layers = []
            for e in range(low, high):
                p = e - spread * tap
                layers.append(grad_at(p if 0 <= p < depth else None))
            columns.append(jnp.concatenate(layers, axis=0))
        rhs = jnp.concatenate(columns, axis=1)
        part = lax.dot_general(lhs, rhs, (((0,), (0,)), ((), ())), preferred_element_type=F32)
        chans = columns[0].shape[1]
        for place, tap in enumerate(depth_taps):
            yield tap, part[:, place * chans : (place + 1) * chans]


def frame_all(store, low_ref, x_ref, high_ref, spread, width, layers=None):
    depth = x_ref.shape[0]
    for layer in range(depth + 2 * spread) if layers is None else layers:
        if layer < spread:
            plane = low_ref[layer]
        elif layer < depth + spread:
            plane = x_ref[layer - spread]
        else:
            plane = high_ref[layer - depth - spread]
        frame(store, layer, plane, spread, width)


def neighbours(count):
    me = lax.axis_index("space")
    return (me > 0, {"space": me - 1}), (me < count - 1, {"space": me + 1})


def greet(peers, ends):
    barrier = pltpu.get_barrier_semaphore()
    for peer in peers:
        pl.semaphore_signal(barrier, inc=1, device_id=peer, device_id_type=pl.DeviceIdType.MESH)
    for exists, peer in ends:

        @pl.when(exists)
        def _(peer=peer):
            pl.semaphore_signal(barrier, inc=1, device_id=peer, device_id_type=pl.DeviceIdType.MESH)

    waits = len(peers)
    if ends:
        me = lax.axis_index("space")
        waits = waits + jnp.minimum(me, 1) + jnp.minimum(lax.axis_size("space") - 1 - me, 1)
    pl.semaphore_wait(barrier, waits)


class Faces:
    def __init__(self, ends, head, tail, low, high, send, recv):
        (self.below, down), (self.above, up) = ends
        self.low, self.high = low, high
        self.down = pltpu.make_async_remote_copy(
            src_ref=head, dst_ref=high, send_sem=send.at[0], recv_sem=recv.at[0],
            device_id=down, device_id_type=pl.DeviceIdType.MESH,
        )
        self.up = pltpu.make_async_remote_copy(
            src_ref=tail, dst_ref=low, send_sem=send.at[1], recv_sem=recv.at[1],
            device_id=up, device_id_type=pl.DeviceIdType.MESH,
        )

    def start(self):
        pl.when(self.below)(self.down.start)
        pl.when(self.above)(self.up.start)

    def finish(self):
        @pl.when(self.below)
        def _():
            self.down.wait_send()
            self.up.wait_recv()

        @pl.when(jnp.logical_not(self.below))
        def _():
            self.low[...] = jnp.zeros(self.low.shape, self.low.dtype)

        @pl.when(self.above)
        def _():
            self.up.wait_send()
            self.down.wait_recv()

        @pl.when(jnp.logical_not(self.above))
        def _():
            self.high[...] = jnp.zeros(self.high.shape, self.high.dtype)


class Total:
    def __init__(self, order, start, size, held, landing, full, send, recv):
        self.held, self.landing, self.full, self.send, self.recv = held, landing, full, send, recv
        base = start
        self.plan = []
        for axis, low, members in order:
            me = lax.axis_index(axis)
            place = lax.rem(me // low, members)
            part = size // members
            others = []
            for step in range(1, members):
                other = lax.rem(place + step, members)
                others.append(({axis: me + (other - place) * low}, start + other * part, base))
                base += part
            start, size = start + place * part, part
            self.plan.append((others, start, part))
        self.copies, self.turn = [], -1

    def rows(self, start, size):
        return pl.ds(pl.multiple_of(start, 16), size)

    def advance(self):
        if self.turn == 2 * len(self.plan):
            return
        if self.turn >= 0:
            self.end(self.turn)
        self.turn += 1
        if self.turn < 2 * len(self.plan):
            self.begin(self.turn)

    def begin(self, turn):
        count = len(self.plan)
        scatter = turn < count
        others, keep, part = self.plan[turn if scatter else 2 * count - 1 - turn]
        if turn == count:
            self.full[self.rows(keep, part)] = self.held[self.rows(keep, part)]
        self.copies = []
        for place, (peer, away, base) in enumerate(others):
            if scatter:
                src, dst = self.held.at[self.rows(away, part)], self.landing.at[pl.ds(base, part)]
            else:
                src = dst = self.full.at[self.rows(keep, part)]
            copy = pltpu.make_async_remote_copy(
                src_ref=src, dst_ref=dst, send_sem=self.send.at[turn, place], recv_sem=self.recv.at[turn, place],
                device_id=peer, device_id_type=pl.DeviceIdType.MESH,
            )
            copy.start()
            self.copies.append(copy)

    def end(self, turn):
        for copy in self.copies:
            copy.wait()
        if turn < len(self.plan):
            others, keep, part = self.plan[turn]
            span = self.rows(keep, part)
            value = self.held[span].astype(F32)
            for _, _, base in others:
                value = value + self.landing[pl.ds(base, part)].astype(F32)
            self.held[span] = value.astype(BF16)


def stages(axis, first, last):
    made = []
    while first < last:
        bits = min(2, last - first)
        made.append((axis, 1 << first, 1 << bits))
        first += bits
    return made


def sum_orders(count, slabs):
    bits = count.bit_length() - 1
    core = stages("sample", 0, min(1, bits))
    near = stages("sample", min(1, bits), min(2, bits))
    far = stages("sample", min(2, bits), bits)
    spaces = stages("space", 0, slabs.bit_length() - 1)
    return core + near + spaces + far, core + spaces + near + far


def whole_body(
    count, slabs, width, partner_ref, share_ref, x_ref, kernel_one_ref, kernel_two_ref, cot_ref,
    result_ref, out_one, out_two,
    got_a, got_b, stage, hidden, mate_ref, faces_one, faces_two, mixed_ref, grad_ref, slope_own_ref, slope_mate_ref,
    store_own, store_mate, store_mix, store_grad, wide_one, wide_two, wide_back, term_own, term_mate, total,
    held_one, held_two, land_one, land_two, full_one, full_two,
    send_one, recv_one, send_two, recv_two, send_face, recv_face, send, recv,
):
    depth, cells, chans = x_ref.shape
    me = lax.axis_index("sample")
    peers = [lax.rem(me + step, count) for step in range(1, count)]
    ends = neighbours(slabs)
    orders = sum_orders(count, slabs)
    far = []
    for axis, low, members in orders[0]:
        if axis == "space":
            at = lax.axis_index(axis)
            place = lax.rem(at // low, members)
            far += [{axis: at + (lax.rem(place + step, members) - place) * low} for step in range(1, members)]
    greet([{"sample": peer} for peer in peers] + far, ends)
    got = (got_a, got_b)
    piece = depth * cells // count
    per_layer = cells // piece
    rows = piece // 2

    def span(index, part):
        return index // per_layer, pl.ds(pl.multiple_of(lax.rem(index, per_layer) * piece + part * rows, 16), rows)

    def push(src, dst, send, recv, peer):
        return pltpu.make_async_remote_copy(
            src_ref=src, dst_ref=dst, send_sem=send, recv_sem=recv,
            device_id={"sample": peer}, device_id_type=pl.DeviceIdType.MESH,
        )

    def faces(block, edge, low, high, kind):
        return Faces(
            ends, block.at[pl.ds(0, edge)], block.at[pl.ds(depth - edge, edge)], low, high,
            send_face.at[kind], recv_face.at[kind],
        )

    own_low, own_high, mate_low, mate_high = [faces_one.at[pl.ds(k, 1)] for k in range(4)]
    mix_low, mix_high, grad_low, grad_high = [faces_two.at[pl.ds(2 * k, 2)] for k in range(4)]

    first, second = [], []
    for part in range(2):
        first.append([
            push(x_ref.at[span(peer, part)], got[part].at[me], send_one.at[part, place], recv_one.at[part, place], peer)
            for place, peer in enumerate(peers)
        ])
        for copy in first[part]:
            copy.start()
        if part == 0:
            own = faces(x_ref, 1, own_low, own_high, 0)
            own.start()
    share = share_ref[me]
    fill_pairs(kernel_one_ref, wide_one)
    frame_all(store_own, None, x_ref, None, 1, width, range(1, depth + 1))
    for part in range(2):
        got[part][me] = x_ref[span(me, part)]
        for copy in first[part]:
            copy.wait_recv()
        second.append([])
        for place, peer in enumerate(peers):
            stage[part, place] = got[part][partner_ref[peer]]
            copy = push(
                stage.at[part, place], mate_ref.at[span(me, part)],
                send_two.at[part, place], recv_two.at[part, place], peer,
            )
            copy.start()
            second[part].append(copy)
        mate_ref[span(me, part)] = got[part][partner_ref[me]]

    own.finish()
    frame_all(store_own, own_low, x_ref, own_high, 1, width, (0, depth + 1))
    for p, value in conv_pairs(store_own, wide_one, groups(depth, 1), 1, width, cells):
        squash = jax.nn.sigmoid(value)
        hidden[p] = (value * squash).astype(BF16)
        slope_own_ref[p] = share * (squash * (1.0 + value * (1.0 - squash)))
    fill_pairs(kernel_two_ref, wide_two)
    fill_back(kernel_two_ref, wide_back)
    for copies in second:
        for copy in copies:
            copy.wait_recv()
    mates = faces(mate_ref, 1, mate_low, mate_high, 1)
    mates.start()
    frame_all(store_mate, None, mate_ref, None, 1, width, range(1, depth + 1))
    mates.finish()
    frame_all(store_mate, mate_low, mate_ref, mate_high, 1, width, (0, depth + 1))

    def mix(pairs):
        for p, value in conv_pairs(store_mate, wide_one, pairs, 1, width, cells):
            squash = jax.nn.sigmoid(value)
            other = (value * squash).astype(BF16).astype(F32)
            mixed_ref[p] = (share * hidden[p].astype(F32) + (1.0 - share) * other).astype(BF16)
            slope_mate_ref[p] = (1.0 - share) * (squash * (1.0 + value * (1.0 - squash)))

    pairs = groups(depth, 1)
    mix([pairs[0], pairs[-1]])
    mixes = faces(mixed_ref, 2, mix_low, mix_high, 2)
    mixes.start()
    mix(pairs[1:-1])
    frame_all(store_mix, None, mixed_ref, None, 2, width, range(2, depth + 2))
    for copies in first + second:
        for copy in copies:
            copy.wait_send()
    mixes.finish()
    frame_all(store_mix, mix_low, mixed_ref, mix_high, 2, width, (0, 1, depth + 2, depth + 3))

    for p, value in conv_pairs(store_mix, wide_two, groups(depth, 2), 2, width, cells):
        squash = jax.nn.sigmoid(value)
        result_ref[p] = (value * squash).astype(BF16)
        grad_ref[p] = (cot_ref[p].astype(F32) * (squash * (1.0 + value * (1.0 - squash)))).astype(BF16)
    backs = faces(grad_ref, 2, grad_low, grad_high, 3)
    backs.start()

    size = held_one.shape[0]
    used = 27 * chans
    unit = 16 * count * slabs
    cut = (size // unit + 1) // 2 * unit

    def lanes(kind, held, land, full):
        made = []
        for lane, (start, end) in enumerate(((0, cut), (cut, size))):
            if end > start:
                made.append(
                    Total(orders[lane], start, end - start, held, land, full, send.at[kind, lane], recv.at[kind, lane])
                )
        return made

    def advance(made):
        for lane in made:
            lane.advance()

    def hand_over(held):
        for tap in range(3):
            held[pl.ds(tap * 9 * chans, 9 * chans)] = total[tap].astype(BF16)
        if size > used:
            held[pl.ds(used, size - used)] = jnp.zeros((size - used, chans), BF16)

    def grad_at(ref, p):
        return jnp.zeros((cells, chans), BF16) if p is None else ref[p]

    def gather(store, term, spread, fresh):
        for place, (tap, part) in enumerate(
            grad_blocks(store, functools.partial(grad_at, term), depth, spread, width, cells)
        ):
            if fresh and place < 3:
                total[tap] = part
            else:
                total[tap] += part
            if place == 2:
                yield

    for _ in gather(store_mix, grad_ref, 2, True):
        pass
    hand_over(held_two)
    seconds = lanes(1, held_two, land_two, full_two)
    advance(seconds)
    frame_all(store_grad, None, grad_ref, None, 2, width, range(2, depth + 2))
    backs.finish()
    frame_all(store_grad, grad_low, grad_ref, grad_high, 2, width, (0, 1, depth + 2, depth + 3))
    for p, value in conv_pairs(store_grad, wide_back, groups(depth, 2), 2, width, cells, back=True):
        value = value.astype(BF16).astype(F32)
        term_own[p] = (value * slope_own_ref[p]).astype(BF16)
        term_mate[p] = (value * slope_mate_ref[p]).astype(BF16)
    advance(seconds)
    for _ in gather(store_own, term_own, 1, True):
        pass
    advance(seconds)
    for _ in gather(store_mate, term_mate, 1, False):
        advance(seconds)
    advance(seconds)
    hand_over(held_one)
    firsts = lanes(0, held_one, land_one, full_one)
    for _ in range(2 * len(orders[0]) + 1):
        advance(firsts)
        advance(seconds)
    out_one[...] = full_one[pl.ds(0, used)].astype(F32)
    out_two[...] = full_two[pl.ds(0, used)].astype(F32)


def whole_call(args, count, slabs, width):
    depth, cells, chans = args[2].shape
    rows = depth * cells // count // 2
    used = 27 * chans
    size = used + -used % (16 * count * slabs)
    turns = 2 * len(sum_orders(count, slabs)[0])
    vmem = pl.BlockSpec(memory_space=pltpu.VMEM)
    smem = pl.BlockSpec(memory_space=pltpu.SMEM)
    dma = pltpu.SemaphoreType.DMA
    slab = pltpu.VMEM((depth, cells, chans), BF16)
    wide_slab = pltpu.VMEM((depth, cells, chans), F32)
    sums = jax.ShapeDtypeStruct((used, chans), F32)
    return pl.pallas_call(
        functools.partial(whole_body, count, slabs, width),
        out_shape=[jax.ShapeDtypeStruct((depth, cells, chans), BF16), sums, sums],
        in_specs=[smem, smem] + [vmem] * 4,
        out_specs=[vmem] * 3,
        scratch_shapes=[
            pltpu.VMEM((count, rows, chans), BF16),
            pltpu.VMEM((count, rows, chans), BF16),
            pltpu.VMEM((2, count - 1, rows, chans), BF16),
            slab,
            slab,
            pltpu.VMEM((4, cells, chans), BF16),
            pltpu.VMEM((8, cells, chans), BF16),
            slab,
            slab,
            wide_slab,
            wide_slab,
            pltpu.VMEM((depth + 2, cells + 2 * width, 3 * chans), BF16),
            pltpu.VMEM((depth + 2, cells + 2 * width, 3 * chans), BF16),
            pltpu.VMEM((depth + 4, cells + 4 * width, 3 * chans), BF16),
            pltpu.VMEM((depth + 4, cells + 4 * width, 3 * chans), BF16),
            pltpu.VMEM((4, 9 * chans, 2 * chans), BF16),
            pltpu.VMEM((4, 9 * chans, 2 * chans), BF16),
            pltpu.VMEM((4, 2 * chans, 9 * chans), BF16),
            slab,
            slab,
            pltpu.VMEM((3, 9 * chans, chans), F32),
        ]
        + [pltpu.VMEM((size, chans), BF16)] * 6
        + [dma((2, count - 1))] * 4
        + [dma((4, 2))] * 2
        + [dma((2, 2, turns, 3))] * 2,
        compiler_params=pltpu.CompilerParams(
            collective_id=0, has_side_effects=True, vmem_limit_bytes=VMEM_LIMIT
        ),
    )(*args)


def shards(volume, first_kernel, second_kernel, partner, coefficient, out_grad):
    _, depth, height, width, chans = volume.shape
    cells = height * width
    count, slabs = lax.axis_size("sample"), lax.axis_size("space")
    result, first_sum, second_sum = whole_call(
        (
            partner,
            coefficient,
            volume.reshape(depth, cells, chans),
            first_kernel.reshape(3, 9 * chans, chans),
            second_kernel.reshape(3, 9 * chans, chans),
            out_grad.reshape(depth, cells, chans),
        ),
        count,
        slabs,
        width,
    )
    shape = first_kernel.shape
    return (
        result.reshape(volume.shape),
        first_sum.reshape(shape),
        second_sum.reshape(shape),
    )


def solution(mesh):
    in_specs = (
        P("sample", "space", None, None, None),
        P(),
        P(),
        P(),
        P(),
        P("sample", "space", None, None, None),
    )
    out_specs = (P("sample", "space", None, None, None), P(), P())
    return jax.shard_map(shards, mesh=mesh, in_specs=in_specs, out_specs=out_specs, check_vma=False)
```

```python
import functools

import jax
import jax.numpy as jnp
from jax import lax
from jax.experimental import pallas as pl
from jax.experimental.pallas import tpu as pltpu
from jax.sharding import PartitionSpec as P

F32 = jnp.float32
BF16 = jnp.bfloat16
VMEM_LIMIT = 56 * 1024 * 1024


def slope(value):
    squash = jax.nn.sigmoid(value)
    return squash * (1.0 + value * (1.0 - squash))


def groups(depth, spread):
    return [p for p in range(depth) if (p // spread) % 2 == 0]


def frame(store, layer, plane, spread, width):
    cells, chans = plane.shape
    edge = spread * width
    wide = plane.astype(F32)
    column = lax.broadcasted_iota(jnp.int32, plane.shape, 0) % width
    left = jnp.where(column >= spread, pltpu.roll(wide, spread, 0), 0.0).astype(BF16)
    right = jnp.where(column < width - spread, pltpu.roll(wide, cells - spread, 0), 0.0).astype(BF16)
    store[layer, pl.ds(0, edge), :] = jnp.zeros((edge, 3 * chans), BF16)
    store[layer, pl.ds(edge + cells, edge), :] = jnp.zeros((edge, 3 * chans), BF16)
    for place, value in enumerate((left, plane, right)):
        store[layer, pl.ds(edge, cells), pl.ds(place * chans, chans)] = value


def taps(store, layer, spread, width, cells):
    return jnp.concatenate(
        [store[layer, pl.ds(row * spread * width, cells), :] for row in range(3)], axis=1
    )


def fill_pairs(kernel_ref, wide_ref):
    chans = kernel_ref.shape[2]
    for step in range(4):
        for out in range(2):
            depth_tap = step - out
            block = (
                kernel_ref[depth_tap]
                if 0 <= depth_tap < 3
                else jnp.zeros(kernel_ref.shape[1:], BF16)
            )
            wide_ref[step, :, pl.ds(out * chans, chans)] = block


def fill_back(kernel_ref, wide_ref):
    chans = kernel_ref.shape[2]
    for step in range(4):
        for out in range(2):
            depth_tap = step - out
            for place in range(9):
                block = (
                    kernel_ref[2 - depth_tap, pl.ds((8 - place) * chans, chans)]
                    if 0 <= depth_tap < 3
                    else jnp.zeros((chans, chans), BF16)
                )
                wide_ref[step, pl.ds(out * chans, chans), pl.ds(place * chans, chans)] = block


def conv_pairs(store, wide_ref, pairs, spread, width, cells, back=False):
    for at in range(0, len(pairs), 2):
        yield from conv_chunk(store, wide_ref, pairs[at : at + 2], spread, width, cells, back)


def conv_chunk(store, wide_ref, first, spread, width, cells, back):
    side = 1 if back else 0
    total = None
    for half in range(2):
        rows = []
        for p in first:
            rows.append(
                jnp.concatenate(
                    [
                        taps(store, p + spread * (2 * half + k), spread, width, cells)
                        for k in range(2)
                    ],
                    axis=1,
                )
            )
        lhs = jnp.concatenate(rows, axis=0)
        rhs = jnp.concatenate([wide_ref[2 * half], wide_ref[2 * half + 1]], axis=side)
        part = lax.dot_general(lhs, rhs, (((1,), (side,)), ((), ())), preferred_element_type=F32)
        total = part if total is None else total + part
    chans = total.shape[1] // 2
    for place, p in enumerate(first):
        for out in range(2):
            yield p + out * spread, total[
                place * cells : (place + 1) * cells, out * chans : (out + 1) * chans
            ]


def grad_blocks(store, grad_at, depth, spread, width, cells):
    ranges = ((2 * spread, depth, (0, 1, 2)), (0, 2 * spread, (0, 1)), (depth, depth + 2 * spread, (1, 2)))
    for low, high, depth_taps in ranges:
        lhs = jnp.concatenate(
            [taps(store, e, spread, width, cells) for e in range(low, high)], axis=0
        )
        columns = []
        for tap in depth_taps:
            layers = []
            for e in range(low, high):
                p = e - spread * tap
                layers.append(grad_at(p if 0 <= p < depth else None))
            columns.append(jnp.concatenate(layers, axis=0))
        rhs = jnp.concatenate(columns, axis=1)
        part = lax.dot_general(lhs, rhs, (((0,), (0,)), ((), ())), preferred_element_type=F32)
        chans = columns[0].shape[1]
        for place, tap in enumerate(depth_taps):
            yield tap, part[:, place * chans : (place + 1) * chans]


def frame_all(store, low_ref, x_ref, high_ref, spread, width, layers=None):
    depth = x_ref.shape[0]
    for layer in range(depth + 2 * spread) if layers is None else layers:
        if layer < spread:
            plane = low_ref[layer]
        elif layer < depth + spread:
            plane = x_ref[layer - spread]
        else:
            plane = high_ref[layer - depth - spread]
        frame(store, layer, plane, spread, width)


def neighbours(count):
    me = lax.axis_index("space")
    return (me > 0, {"space": me - 1}), (me < count - 1, {"space": me + 1})


def greet(peers, ends):
    barrier = pltpu.get_barrier_semaphore()
    for peer in peers:
        pl.semaphore_signal(barrier, inc=1, device_id=peer, device_id_type=pl.DeviceIdType.MESH)
    for exists, peer in ends:

        @pl.when(exists)
        def _(peer=peer):
            pl.semaphore_signal(barrier, inc=1, device_id=peer, device_id_type=pl.DeviceIdType.MESH)

    waits = len(peers)
    if ends:
        me = lax.axis_index("space")
        waits = waits + jnp.minimum(me, 1) + jnp.minimum(lax.axis_size("space") - 1 - me, 1)
    pl.semaphore_wait(barrier, waits)


class Faces:
    def __init__(self, ends, head, tail, low, high, send, recv):
        (self.below, down), (self.above, up) = ends
        self.low, self.high = low, high
        self.down = pltpu.make_async_remote_copy(
            src_ref=head, dst_ref=high, send_sem=send.at[0], recv_sem=recv.at[0],
            device_id=down, device_id_type=pl.DeviceIdType.MESH,
        )
        self.up = pltpu.make_async_remote_copy(
            src_ref=tail, dst_ref=low, send_sem=send.at[1], recv_sem=recv.at[1],
            device_id=up, device_id_type=pl.DeviceIdType.MESH,
        )

    def start(self):
        pl.when(self.below)(self.down.start)
        pl.when(self.above)(self.up.start)

    def finish(self):
        @pl.when(self.below)
        def _():
            self.down.wait_send()
            self.up.wait_recv()

        @pl.when(jnp.logical_not(self.below))
        def _():
            self.low[...] = jnp.zeros(self.low.shape, self.low.dtype)

        @pl.when(self.above)
        def _():
            self.up.wait_send()
            self.down.wait_recv()

        @pl.when(jnp.logical_not(self.above))
        def _():
            self.high[...] = jnp.zeros(self.high.shape, self.high.dtype)


class Total:
    def __init__(self, order, start, size, held, landing, full, send, recv):
        self.held, self.landing, self.full, self.send, self.recv = held, landing, full, send, recv
        base = start
        self.plan = []
        for axis, low, members in order:
            me = lax.axis_index(axis)
            place = lax.rem(me // low, members)
            part = size // members
            others = []
            for step in range(1, members):
                other = lax.rem(place + step, members)
                others.append(({axis: me + (other - place) * low}, start + other * part, base))
                base += part
            start, size = start + place * part, part
            self.plan.append((others, start, part))
        self.copies, self.turn = [], -1

    def rows(self, start, size):
        return pl.ds(pl.multiple_of(start, 16), size)

    def advance(self):
        if self.turn == 2 * len(self.plan):
            return
        if self.turn >= 0:
            self.end(self.turn)
        self.turn += 1
        if self.turn < 2 * len(self.plan):
            self.begin(self.turn)

    def begin(self, turn):
        count = len(self.plan)
        scatter = turn < count
        others, keep, part = self.plan[turn if scatter else 2 * count - 1 - turn]
        if turn == count:
            self.full[self.rows(keep, part)] = self.held[self.rows(keep, part)]
        self.copies = []
        for place, (peer, away, base) in enumerate(others):
            if scatter:
                src, dst = self.held.at[self.rows(away, part)], self.landing.at[pl.ds(base, part)]
            else:
                src = dst = self.full.at[self.rows(keep, part)]
            copy = pltpu.make_async_remote_copy(
                src_ref=src, dst_ref=dst, send_sem=self.send.at[turn, place], recv_sem=self.recv.at[turn, place],
                device_id=peer, device_id_type=pl.DeviceIdType.MESH,
            )
            copy.start()
            self.copies.append(copy)

    def end(self, turn):
        for copy in self.copies:
            copy.wait()
        if turn < len(self.plan):
            others, keep, part = self.plan[turn]
            span = self.rows(keep, part)
            value = self.held[span].astype(F32)
            for _, _, base in others:
                value = value + self.landing[pl.ds(base, part)].astype(F32)
            self.held[span] = value.astype(BF16)


def stages(axis, first, last):
    made = []
    while first < last:
        bits = min(2, last - first)
        made.append((axis, 1 << first, 1 << bits))
        first += bits
    return made


def sum_orders(count, slabs):
    bits = count.bit_length() - 1
    core = stages("sample", 0, min(1, bits))
    near = stages("sample", min(1, bits), min(2, bits))
    far = stages("sample", min(2, bits), bits)
    spaces = stages("space", 0, slabs.bit_length() - 1)
    return core + near + spaces + far, core + spaces + near + far


def whole_body(
    count, slabs, width, partner_ref, share_ref, x_ref, kernel_one_ref, kernel_two_ref, cot_ref,
    result_ref, out_one, out_two,
    got_a, got_b, stage, hidden, mate_ref, faces_one, faces_two, mixed_ref, grad_ref, slope_own_ref, slope_mate_ref,
    store_own, store_mate, store_mix, store_grad, wide_one, wide_two, wide_back, term_own, term_mate, total,
    held_one, held_two, land_one, land_two, full_one, full_two,
    send_one, recv_one, send_two, recv_two, send_face, recv_face, send, recv,
):
    depth, cells, chans = x_ref.shape
    me = lax.axis_index("sample")
    peers = [lax.rem(me + step, count) for step in range(1, count)]
    ends = neighbours(slabs)
    orders = sum_orders(count, slabs)
    far = []
    for axis, low, members in orders[0]:
        if axis == "space":
            at = lax.axis_index(axis)
            place = lax.rem(at // low, members)
            far += [{axis: at + (lax.rem(place + step, members) - place) * low} for step in range(1, members)]
    greet([{"sample": peer} for peer in peers] + far, ends)
    got = (got_a, got_b)
    piece = depth * cells // count
    per_layer = cells // piece
    rows = piece // 2

    def span(index, part):
        return index // per_layer, pl.ds(pl.multiple_of(lax.rem(index, per_layer) * piece + part * rows, 16), rows)

    def push(src, dst, send, recv, peer):
        return pltpu.make_async_remote_copy(
            src_ref=src, dst_ref=dst, send_sem=send, recv_sem=recv,
            device_id={"sample": peer}, device_id_type=pl.DeviceIdType.MESH,
        )

    def faces(block, edge, low, high, kind):
        return Faces(
            ends, block.at[pl.ds(0, edge)], block.at[pl.ds(depth - edge, edge)], low, high,
            send_face.at[kind], recv_face.at[kind],
        )

    own_low, own_high, mate_low, mate_high = [faces_one.at[pl.ds(k, 1)] for k in range(4)]
    mix_low, mix_high, grad_low, grad_high = [faces_two.at[pl.ds(2 * k, 2)] for k in range(4)]

    first, second = [], []
    for part in range(2):
        first.append([
            push(x_ref.at[span(peer, part)], got[part].at[me], send_one.at[part, place], recv_one.at[part, place], peer)
            for place, peer in enumerate(peers)
        ])
        for copy in first[part]:
            copy.start()
        if part == 0:
            own = faces(x_ref, 1, own_low, own_high, 0)
            own.start()
    share = share_ref[me]
    fill_pairs(kernel_one_ref, wide_one)
    frame_all(store_own, None, x_ref, None, 1, width, range(1, depth + 1))
    for part in range(2):
        got[part][me] = x_ref[span(me, part)]
        for copy in first[part]:
            copy.wait_recv()
        second.append([])
        for place, peer in enumerate(peers):
            stage[part, place] = got[part][partner_ref[peer]]
            copy = push(
                stage.at[part, place], mate_ref.at[span(me, part)],
                send_two.at[part, place], recv_two.at[part, place], peer,
            )
            copy.start()
            second[part].append(copy)
        mate_ref[span(me, part)] = got[part][partner_ref[me]]

    own.finish()
    frame_all(store_own, own_low, x_ref, own_high, 1, width, (0, depth + 1))
    for p, value in conv_pairs(store_own, wide_one, groups(depth, 1), 1, width, cells):
        squash = jax.nn.sigmoid(value)
        hidden[p] = (value * squash).astype(BF16)
        slope_own_ref[p] = share * (squash * (1.0 + value * (1.0 - squash)))
    fill_pairs(kernel_two_ref, wide_two)
    fill_back(kernel_two_ref, wide_back)
    for copies in second:
        for copy in copies:
            copy.wait_recv()
    mates = faces(mate_ref, 1, mate_low, mate_high, 1)
    mates.start()
    frame_all(store_mate, None, mate_ref, None, 1, width, range(1, depth + 1))
    mates.finish()
    frame_all(store_mate, mate_low, mate_ref, mate_high, 1, width, (0, depth + 1))

    def mix(pairs):
        for p, value in conv_pairs(store_mate, wide_one, pairs, 1, width, cells):
            squash = jax.nn.sigmoid(value)
            other = (value * squash).astype(BF16).astype(F32)
            mixed_ref[p] = (share * hidden[p].astype(F32) + (1.0 - share) * other).astype(BF16)
            slope_mate_ref[p] = (1.0 - share) * (squash * (1.0 + value * (1.0 - squash)))

    pairs = groups(depth, 1)
    mix([pairs[0], pairs[-1]])
    mixes = faces(mixed_ref, 2, mix_low, mix_high, 2)
    mixes.start()
    mix(pairs[1:-1])
    frame_all(store_mix, None, mixed_ref, None, 2, width, range(2, depth + 2))
    for copies in first + second:
        for copy in copies:
            copy.wait_send()
    mixes.finish()
    frame_all(store_mix, mix_low, mixed_ref, mix_high, 2, width, (0, 1, depth + 2, depth + 3))

    for p, value in conv_pairs(store_mix, wide_two, groups(depth, 2), 2, width, cells):
        squash = jax.nn.sigmoid(value)
        result_ref[p] = (value * squash).astype(BF16)
        grad_ref[p] = (cot_ref[p].astype(F32) * (squash * (1.0 + value * (1.0 - squash)))).astype(BF16)
    backs = faces(grad_ref, 2, grad_low, grad_high, 3)
    backs.start()

    size = held_one.shape[0]
    used = 27 * chans
    unit = 16 * count * slabs
    cut = (size // unit + 1) // 2 * unit

    def lanes(kind, held, land, full):
        made = []
        for lane, (start, end) in enumerate(((0, cut), (cut, size))):
            if end > start:
                made.append(
                    Total(orders[lane], start, end - start, held, land, full, send.at[kind, lane], recv.at[kind, lane])
                )
        return made

    def advance(made):
        for lane in made:
            lane.advance()

    def hand_over(held):
        for tap in range(3):
            held[pl.ds(tap * 9 * chans, 9 * chans)] = total[tap].astype(BF16)
        if size > used:
            held[pl.ds(used, size - used)] = jnp.zeros((size - used, chans), BF16)

    def grad_at(ref, p):
        return jnp.zeros((cells, chans), BF16) if p is None else ref[p]

    def gather(store, term, spread, fresh):
        for place, (tap, part) in enumerate(
            grad_blocks(store, functools.partial(grad_at, term), depth, spread, width, cells)
        ):
            if fresh and place < 3:
                total[tap] = part
            else:
                total[tap] += part
            if place == 2:
                yield

    for _ in gather(store_mix, grad_ref, 2, True):
        pass
    hand_over(held_two)
    seconds = lanes(1, held_two, land_two, full_two)
    advance(seconds)
    frame_all(store_grad, None, grad_ref, None, 2, width, range(2, depth + 2))
    backs.finish()
    frame_all(store_grad, grad_low, grad_ref, grad_high, 2, width, (0, 1, depth + 2, depth + 3))
    for p, value in conv_pairs(store_grad, wide_back, groups(depth, 2), 2, width, cells, back=True):
        value = value.astype(BF16).astype(F32)
        term_own[p] = (value * slope_own_ref[p]).astype(BF16)
        term_mate[p] = (value * slope_mate_ref[p]).astype(BF16)
    advance(seconds)
    for _ in gather(store_own, term_own, 1, True):
        pass
    advance(seconds)
    for _ in gather(store_mate, term_mate, 1, False):
        advance(seconds)
    advance(seconds)
    hand_over(held_one)
    firsts = lanes(0, held_one, land_one, full_one)
    for _ in range(2 * len(orders[0]) + 1):
        advance(firsts)
        advance(seconds)
    out_one[...] = full_one[pl.ds(0, used)]
    out_two[...] = full_two[pl.ds(0, used)]


def whole_call(args, count, slabs, width):
    depth, cells, chans = args[2].shape
    rows = depth * cells // count // 2
    used = 27 * chans
    size = used + -used % (16 * count * slabs)
    turns = 2 * len(sum_orders(count, slabs)[0])
    vmem = pl.BlockSpec(memory_space=pltpu.VMEM)
    smem = pl.BlockSpec(memory_space=pltpu.SMEM)
    dma = pltpu.SemaphoreType.DMA
    slab = pltpu.VMEM((depth, cells, chans), BF16)
    wide_slab = pltpu.VMEM((depth, cells, chans), F32)
    sums = jax.ShapeDtypeStruct((used, chans), BF16)
    return pl.pallas_call(
        functools.partial(whole_body, count, slabs, width),
        out_shape=[jax.ShapeDtypeStruct((depth, cells, chans), BF16), sums, sums],
        in_specs=[smem, smem] + [vmem] * 4,
        out_specs=[vmem] * 3,
        scratch_shapes=[
            pltpu.VMEM((count, rows, chans), BF16),
            pltpu.VMEM((count, rows, chans), BF16),
            pltpu.VMEM((2, count - 1, rows, chans), BF16),
            slab,
            slab,
            pltpu.VMEM((4, cells, chans), BF16),
            pltpu.VMEM((8, cells, chans), BF16),
            slab,
            slab,
            wide_slab,
            wide_slab,
            pltpu.VMEM((depth + 2, cells + 2 * width, 3 * chans), BF16),
            pltpu.VMEM((depth + 2, cells + 2 * width, 3 * chans), BF16),
            pltpu.VMEM((depth + 4, cells + 4 * width, 3 * chans), BF16),
            pltpu.VMEM((depth + 4, cells + 4 * width, 3 * chans), BF16),
            pltpu.VMEM((4, 9 * chans, 2 * chans), BF16),
            pltpu.VMEM((4, 9 * chans, 2 * chans), BF16),
            pltpu.VMEM((4, 2 * chans, 9 * chans), BF16),
            slab,
            slab,
            pltpu.VMEM((3, 9 * chans, chans), F32),
        ]
        + [pltpu.VMEM((size, chans), BF16)] * 6
        + [dma((2, count - 1))] * 4
        + [dma((4, 2))] * 2
        + [dma((2, 2, turns, 3))] * 2,
        compiler_params=pltpu.CompilerParams(
            collective_id=0, has_side_effects=True, vmem_limit_bytes=VMEM_LIMIT
        ),
    )(*args)


def shards(volume, first_kernel, second_kernel, partner, coefficient, out_grad):
    _, depth, height, width, chans = volume.shape
    cells = height * width
    count, slabs = lax.axis_size("sample"), lax.axis_size("space")
    result, first_sum, second_sum = whole_call(
        (
            partner,
            coefficient,
            volume.reshape(depth, cells, chans),
            first_kernel.reshape(3, 9 * chans, chans),
            second_kernel.reshape(3, 9 * chans, chans),
            out_grad.reshape(depth, cells, chans),
        ),
        count,
        slabs,
        width,
    )
    shape = first_kernel.shape
    return (
        result.reshape(volume.shape),
        first_sum.astype(F32).reshape(shape),
        second_sum.astype(F32).reshape(shape),
    )


def solution(mesh):
    in_specs = (
        P("sample", "space", None, None, None),
        P(),
        P(),
        P(),
        P(),
        P("sample", "space", None, None, None),
    )
    out_specs = (P("sample", "space", None, None, None), P(), P())
    return jax.shard_map(shards, mesh=mesh, in_specs=in_specs, out_specs=out_specs, check_vma=False)
```
